512 devices in a mesh: group: 16 (over z_hi, y, core), dp: 32 (over z_lo, x).
Axes of the slice: x: 4, y: 4, z: 16 (z_hi: 2, z_lo: 8; z = z_hi * 8 + z_lo), core: 2. Of those that a mesh axis runs over, the one named last changes fastest.
Arguments:
- grad: bfloat16 [16, 64, 512, 512], P('group', 'dp'), may hold values from -6 to 6
- stats: float32 [16, 32, 512, 512], P('group', 'dp'), may hold values from -3584 to 3584, as said below
- owner: int32 [32, 2], replicated, may hold values from 0 to 7, all different within a row
Outputs:
- new_stats: float32 [16, 32, 512, 512], P('group', 'dp')
- update: bfloat16 [64, 512, 512], P('dp')
The draws below stay inside these ranges and needn't reach their ends.
Inputs may be any that keep to these rules, and one draw needn't show every extreme that they name: The entries of a row of owner are different. `stats`: every matrix is symmetric positive definite.
All inputs are finite; a program needn't handle non-finite values.
Results may differ from the reference program's by a relative error of at most 0.03.
Values may be sent and summed in bfloat16 or wider, within the bound.
No kernel may reach another device: no remote copies, remote signals or barrier semaphores. Data moves between devices by JAX's collectives and lax.ppermute only.
A program may use at most 64 MiB of HBM per device.

```python
import jax
import jax.numpy as jnp
from jax import lax

BS = 512
BLK_COL = 2
NEWTON_ITERS = 3
GROUPS = 16
PAIRS = 8
COLUMNS = 32
NBLK = 64


def column_scales(key):
    key = jax.random.fold_in(key, 5)
    keys = jax.random.split(key, 2)
    lowest = jnp.log(0.3)
    highest = jnp.log(3.0)
    row_scale = jnp.exp(jax.random.uniform(keys[0], (COLUMNS, BS), jnp.float32, lowest, highest))
    col_scale = jnp.exp(jax.random.uniform(keys[1], (COLUMNS, BS), jnp.float32, lowest, highest))
    return (row_scale, col_scale)


def draw_grad(key, part):
    row_scale, col_scale = column_scales(key)
    key = jax.random.fold_in(key, 11)
    keys = jax.random.split(key, 3)
    rank = max(BS // 16, 2)
    left_factor = jax.random.normal(keys[0], (NBLK, BS, rank), jnp.float32)
    right_factor = jax.random.normal(keys[1], (NBLK, BS, rank), jnp.float32)
    decay = jnp.exp(-3.0 * jnp.arange(rank, dtype=jnp.float32) / rank)
    decay = decay / jnp.sqrt(jnp.mean(decay * decay))
    common = jnp.einsum('bir,bjr->bij', left_factor * decay, right_factor, precision=lax.Precision.HIGHEST)
    common = jnp.clip(common / jnp.sqrt(jnp.float32(rank)), -4.0, 4.0)
    own = jnp.clip(jax.random.normal(keys[2], (GROUPS, NBLK, BS, BS), jnp.float32), -4.0, 4.0)
    values = 0.5 * common[None] + own
    factor = 0.08
    rows_block = jnp.repeat(row_scale, BLK_COL, axis=0)
    cols_block = jnp.repeat(col_scale, BLK_COL, axis=0)
    scaled = factor * values * rows_block[None, :, :, None] * cols_block[None, :, None, :]
    return scaled.astype(jnp.bfloat16)


def draw_stats(key, part):
    row_scale, col_scale = column_scales(key)
    key = jax.random.fold_in(key, 23)
    keys = jax.random.split(key, 1)
    inner = BS
    factors = jnp.clip(jax.random.normal(keys[0], (GROUPS, COLUMNS, BS, inner), jnp.float32), -3.0, 3.0)
    floor_value = 0.02
    factor = 1.0
    gram = jnp.einsum('gcik,gcjk->gcij', factors, factors, precision=lax.Precision.HIGHEST) / inner
    gram = 0.5 * (gram + jnp.swapaxes(gram, 2, 3))
    even = jnp.arange(GROUPS, dtype=jnp.int32) % 2 == 0
    scales = jnp.sqrt(jnp.where(even[:, None, None], row_scale[None], col_scale[None]))
    eye = jnp.eye(BS, dtype=jnp.float32)
    matrix = factor * BS * scales[..., :, None] * scales[..., None, :] * (gram + floor_value * eye)
    return matrix.astype(jnp.float32)


def picks_of(own_key, rows, amount, top, lift):
    sequence = jax.random.permutation(jax.random.fold_in(own_key, 1), amount)
    boost = sequence
    for power in range(3):
        boost = boost * boost // amount
    boost = boost * lift // amount
    tickets = jax.random.randint(jax.random.fold_in(own_key, 2), (rows, amount), 0, 4096) + boost
    sure = jax.random.permutation(jax.random.fold_in(own_key, 3), rows)[jnp.arange(amount) % rows]
    tickets = jnp.where(jnp.arange(rows)[:, None] == sure[None, :], 1 << 14, tickets)
    merit = tickets * amount + jnp.arange(amount)
    return lax.top_k(merit.astype(jnp.int32), top)[1].astype(jnp.int32)


def setup_inputs(seed: int = 0) -> dict:
    arg_keys = jax.random.split(jax.random.key(seed), 4)
    grad = draw_grad(jax.random.fold_in(arg_keys[3], 71), 0)
    stats = draw_stats(jax.random.fold_in(arg_keys[3], 71), 0)
    owner = picks_of(arg_keys[2], COLUMNS, PAIRS, BLK_COL, 0)
    return dict(grad=grad, stats=stats, owner=owner)


BETA = 0.9
DAMPING = 0.0001

def matmul(left, right):
    return jnp.dot(left, right, precision=lax.Precision.HIGHEST, preferred_element_type=jnp.float32)

def fourth_root(matrix):
    order = matrix.shape[0]
    eye = jnp.eye(order, dtype=jnp.float32)
    shifted = matrix + DAMPING * eye
    frob = jnp.sqrt(jnp.sum(shifted * shifted))
    current = shifted / frob
    result = eye * frob ** (-0.25)
    for step in range(NEWTON_ITERS):
        factor = (5.0 * eye - current) * 0.25
        result = matmul(result, factor)
        if step + 1 < NEWTON_ITERS:
            square = matmul(factor, factor)
            current = matmul(matmul(square, square), current)
    return result

def reference(grad, stats, owner):

    def one_block(index):
        column = index // BLK_COL
        slot = index % BLK_COL
        total = lax.optimization_barrier(jnp.sum(grad[:, index].astype(jnp.float32), axis=0)).astype(jnp.bfloat16)
        pair = owner[column, slot]
        left_old = stats[2 * pair, column]
        right_old = stats[2 * pair + 1, column]
        left_new = BETA * left_old + (1.0 - BETA) * jnp.dot(total, total.T, preferred_element_type=jnp.float32)
        right_new = BETA * right_old + (1.0 - BETA) * jnp.dot(total.T, total, preferred_element_type=jnp.float32)
        dense = total.astype(jnp.float32)
        precond = matmul(matmul(fourth_root(left_new), dense), fourth_root(right_new))
        grad_sq = jnp.sum(dense * dense)
        pre_sq = jnp.sum(precond * precond)
        update = (precond * jnp.sqrt(grad_sq / (pre_sq + 1e-06))).astype(jnp.bfloat16)
        return (left_new, right_new, update)
    lefts, rights, updates = lax.map(one_block, jnp.arange(NBLK, dtype=jnp.int32))
    columns = (jnp.arange(NBLK, dtype=jnp.int32) // BLK_COL).astype(jnp.int32)
    pairs = owner.reshape(-1).astype(jnp.int32)
    new_stats = stats.at[2 * pairs, columns].set(lefts)
    new_stats = new_stats.at[2 * pairs + 1, columns].set(rights)
    return (new_stats, updates)
```

```python
import functools

import jax
import jax.numpy as jnp
from jax import lax
from jax.experimental import pallas as pl
from jax.experimental.pallas import tpu as pltpu
from jax.sharding import PartitionSpec as P

BETA = 0.9
DAMPING = 0.0001
BS = 512
HALF = BS // 2
QUARTER = BS // 8
PACK = 320
PART = PACK // 4
ROWS = 2 * QUARTER
WIDE = ROWS + PART
LIMIT = 32 * 1024 * 1024

BF = jnp.bfloat16
F32 = jnp.float32

VM = pl.BlockSpec(memory_space=pltpu.VMEM)
SM = pl.BlockSpec(memory_space=pltpu.SMEM)


def call(kernel, shapes, specs, scratch=(), flops=0, nbytes=0):
    return pl.pallas_call(
        kernel,
        out_shape=shapes,
        in_specs=specs,
        out_specs=VM,
        scratch_shapes=list(scratch),
        compiler_params=pltpu.CompilerParams(vmem_limit_bytes=LIMIT),
        cost_estimate=pl.CostEstimate(flops=flops, bytes_accessed=nbytes, transcendentals=0),
    )


def mm(a, b):
    return jnp.dot(a.astype(BF), b.astype(BF), preferred_element_type=F32)


def pack_rows(s, out):
    def put(row, col, value):
        rows, cols = value.shape
        done = 0
        while done < rows:
            part, at = divmod(row + done, PART)
            n = min(rows - done, PART - at)
            out[part, ROWS + at : ROWS + at + n, col : col + cols] = value[done : done + n]
            done += n

    put(0, 0, s[0:128, :].astype(BF))
    put(128, 0, s[128:256, 128:512].astype(BF))
    put(128, 384, s[384:512, 384:512].astype(BF))
    put(256, 0, s[256:320, 256:512].astype(BF))
    put(256, 256, s[320:384, 256:512].astype(BF))


def unpack_rows(p, s):
    top = p[0:128, :].astype(F32)
    s[0:128, :] = top
    s[128:512, 0:128] = top[:, 128:512].T
    second = p[128:256, :].astype(F32)
    s[128:256, 128:512] = second[:, 0:384]
    s[256:512, 128:256] = second[:, 128:384].T
    s[384:512, 384:512] = second[:, 384:512]
    s[256:320, 256:512] = p[256:320, 0:256].astype(F32)
    s[320:384, 256:512] = p[256:320, 256:512].astype(F32)
    s[384:512, 256:384] = s[256:384, 384:512].T


def first_kernel(meta, grad, got, stat, out):
    core = meta[0]
    for b in range(2):
        for y in range(4):
            at = pl.multiple_of(core * HALF + y * QUARTER, QUARTER)
            mine = grad[b, pl.ds(at, QUARTER), :].astype(F32)
            other = got[b, y * QUARTER : (y + 1) * QUARTER, :].astype(F32)
            out[y, b * QUARTER : (b + 1) * QUARTER, :] = (mine + other).astype(BF)
    pack_rows(stat, out)


def second_kernel(meta, got, out):
    total = got[0, 0:ROWS, :].astype(F32)
    for y in range(1, 4):
        total += got[y, 0:ROWS, :].astype(F32)
    out[0:ROWS, :] = total.astype(BF)
    for b in range(2):
        out[ROWS + b * PART : ROWS + (b + 1) * PART, :] = got[meta[4 + b], ROWS:WIDE, :]


def third_kernel(meta, mine, got, out):
    total = (mine[0:ROWS, :].astype(F32) + got[0:ROWS, :].astype(F32)).astype(BF)
    for y in range(4):
        out[y, 0:ROWS, :] = total
    for b in range(2):
        here = meta[6 + b] == 1
        lo = ROWS + b * PART
        rows = slice(lo, lo + PART)

        @pl.when(here)
        def _():
            for y in range(2):
                out[2 * b + y, ROWS:WIDE, :] = mine[rows, :]

        @pl.when(jnp.logical_not(here))
        def _():
            for y in range(2):
                out[2 * b + y, ROWS:WIDE, :] = got[rows, :]


def assemble(core, block, mine, other, dense):
    lo = pl.multiple_of(block * QUARTER, QUARTER)
    for y in range(4):
        at = pl.multiple_of(core * HALF + y * QUARTER, QUARTER)
        dense[pl.ds(at, QUARTER), :] = mine[y, pl.ds(lo, QUARTER), :]
        at = pl.multiple_of((1 - core) * HALF + y * QUARTER, QUARTER)
        dense[pl.ds(at, QUARTER), :] = other[y, pl.ds(lo, QUARTER), :]


def gram_of(core, dense, oriented):
    @pl.when(core == 0)
    def _():
        oriented[...] = dense[...]

    @pl.when(core == 1)
    def _():
        oriented[...] = dense[...].astype(F32).T.astype(BF)

    value = oriented[...]
    return lax.dot_general(value, value, (((1,), (1,)), ((), ())), preferred_element_type=F32)


def newton(current):
    low = current.astype(BF)
    square = (1.0 / 16) * mm(low, low) - (10.0 / 16) * current
    slow = square.astype(BF)
    fourth = (50.0 / 16) * square + mm(slow, slow)
    return (625.0 / 256) * current + mm(fourth, low)


def root_kernel(meta, mine, other, out, dense, oriented, packed, stat):
    core = meta[0]
    assemble(core, meta[3], mine, other, dense)
    for y in range(4):
        packed[y * PART : (y + 1) * PART, :] = mine[y, ROWS:WIDE, :]
    unpack_rows(packed, stat)
    gram = gram_of(core, dense, oriented)
    rows = lax.broadcasted_iota(jnp.int32, (BS, BS), 0)
    cols = lax.broadcasted_iota(jnp.int32, (BS, BS), 1)
    shifted = BETA * stat[...] + (1.0 - BETA) * gram + jnp.where(rows == cols, DAMPING, 0.0)
    frob = jnp.sqrt(jnp.sum(shifted * shifted, keepdims=True))
    m0 = shifted * (1.0 / frob)
    m1 = newton(m0)
    m2 = newton(m1)
    n01 = (-1.25 / 4) * (m0 + m1) + (1.0 / 16) * mm(m0, m1)
    excess = 1.25 * n01 - (1.5625 / 4) * m2 - 0.25 * mm(n01, m2)
    scale = lax.rsqrt(jnp.sqrt(frob))

    @pl.when(core == 0)
    def _():
        block = dense[...]
        out[0:BS, :] = (scale * (1.953125 * block.astype(F32) + mm(excess, block))).astype(BF)
        out[BS : BS + 16, :] = jnp.zeros((16, BS), BF)

    @pl.when(core == 1)
    def _():
        out[0:BS, :] = excess.astype(BF)
        value = jnp.broadcast_to(scale, (16, BS))
        high = value.astype(BF).astype(F32)
        middle = (value - high).astype(BF).astype(F32)
        low = value - high - middle
        row = lax.broadcasted_iota(jnp.int32, (16, BS), 0)
        out[BS : BS + 16, :] = jnp.where(row == 0, high, jnp.where(row == 1, middle, low)).astype(BF)


def stat_kernel(meta, mine, other, stat, out, dense, oriented):
    @pl.when(meta[8] == 1)
    def _():
        assemble(meta[0], meta[9], mine, other, dense)
        out[...] = BETA * stat[...] + (1.0 - BETA) * gram_of(meta[0], dense, oriented)

    @pl.when(meta[8] == 0)
    def _():
        out[...] = stat[...]


def product_kernel(meta, mine, other, first, second, out, dense, left, right, prod):
    core = meta[0]
    assemble(core, meta[3], first, second, dense)

    @pl.when(core == 0)
    def _():
        left[...] = mine[...]
        right[...] = other[...]

    @pl.when(core == 1)
    def _():
        left[...] = other[...]
        right[...] = mine[...]

    tail = right[BS : BS + 16, :].astype(F32)
    scale = tail[0:1, 0:1] + tail[1:2, 0:1] + tail[2:3, 0:1]
    low = left[0:BS, :]
    precond = scale * (1.953125 * low.astype(F32) + mm(low, right[0:BS, :]))
    value = dense[...].astype(F32)
    grad_sq = jnp.sum(value * value, keepdims=True)
    pre_sq = jnp.sum(precond * precond, keepdims=True)
    prod[...] = (precond * jnp.sqrt(grad_sq / (pre_sq + 1e-06))).astype(BF)
    at = pl.multiple_of(lax.rem(meta[2], 2) * HALF + core * (HALF // 2), HALF // 2)
    rows = prod[pl.ds(at, HALF // 2), :]
    for y in range(4):
        out[y] = rows


def last_kernel(meta, mine, other, out):
    here = pl.multiple_of(meta[0] * (HALF // 2), HALF // 2)
    there = pl.multiple_of((1 - meta[0]) * (HALF // 2), HALF // 2)
    for y in range(4):
        lo = (y % 2) * HALF
        out[y // 2, pl.ds(lo + here, HALF // 2), :] = mine[y]
        out[y // 2, pl.ds(lo + there, HALF // 2), :] = other[y]


def body(grad, stats, owner):
    group = lax.axis_index("group")
    column = lax.axis_index("dp")
    core, y, half = group % 2, (group // 2) % 4, group // 8
    row = lax.dynamic_index_in_dim(owner, column, 0, keepdims=False)
    matches = (row == group // 2).astype(jnp.int32)
    meta = jnp.stack(
        [
            core,
            half,
            y,
            y // 2,
            row[0] % 4,
            row[1] % 4,
            (row[0] // 4 == half).astype(jnp.int32),
            (row[1] // 4 == half).astype(jnp.int32),
            jnp.max(matches),
            matches[1],
        ]
    ).astype(jnp.int32)
    along_y = [[h * 8 + 2 * k + c for k in range(4)] for h in range(2) for c in range(2)]
    swap = [(g, g ^ 1) for g in range(16)]
    cross = [(g, g ^ 8) for g in range(16)]

    def exchange(value):
        return lax.all_to_all(value, "group", 0, 0, tiled=True, axis_index_groups=along_y)

    block = grad[0]
    stat = stats[0, 0]
    away = lax.dynamic_slice_in_dim(block, (1 - core) * HALF, HALF, 1)
    got = lax.ppermute(away, "group", swap)
    parts = call(first_kernel, jax.ShapeDtypeStruct((4, WIDE, BS), BF), [SM, VM, VM, VM])(meta, block, got, stat)
    parts = exchange(parts)
    mine = call(second_kernel, jax.ShapeDtypeStruct((ROWS + 2 * PART, BS), BF), [SM, VM])(meta, parts)
    got = lax.ppermute(mine, "group", cross)
    parts = call(third_kernel, jax.ShapeDtypeStruct((4, WIDE, BS), BF), [SM, VM, VM])(meta, mine, got)
    parts = exchange(parts)
    other = lax.ppermute(parts[:, :ROWS], "group", swap)
    square = pltpu.VMEM((BS, BS), BF)
    payload = call(
        root_kernel,
        jax.ShapeDtypeStruct((BS + 16, BS), BF),
        [SM, VM, VM],
        [square, square, pltpu.VMEM((PACK, BS), BF), pltpu.VMEM((BS, BS), F32)],
        flops=10 * 2 * BS**3,
    )(meta, parts, other)
    received = lax.ppermute(payload, "group", swap)
    new_stat = call(
        stat_kernel, jax.ShapeDtypeStruct((BS, BS), F32), [SM, VM, VM, VM], [square, square], flops=2 * BS**3, nbytes=3 << 20
    )(meta, parts, other, stat)
    tall = pltpu.VMEM((BS + 16, BS), BF)
    rows = call(
        product_kernel,
        jax.ShapeDtypeStruct((4, HALF // 2, BS), BF),
        [SM, VM, VM, VM, VM],
        [square, tall, tall, square],
        flops=2 * BS**3,
    )(meta, payload, received, parts, other)
    rows = exchange(rows)
    rest = lax.ppermute(rows, "group", swap)
    update = call(last_kernel, jax.ShapeDtypeStruct((2, BS, BS), BF), [SM, VM, VM])(meta, rows, rest)
    return (new_stat[None, None], update)


def solution(mesh):
    in_specs = (P("group", "dp", None, None), P("group", "dp", None, None), P())
    out_specs = (P("group", "dp", None, None), P("dp", None, None))
    return jax.shard_map(body, mesh=mesh, in_specs=in_specs, out_specs=out_specs, check_vma=False)
```

```python
import jax
import jax.numpy as jnp
from jax import lax
from jax.experimental import pallas as pl
from jax.experimental.pallas import tpu as pltpu
from jax.sharding import PartitionSpec as P

BETA = 0.9
DAMPING = 0.0001
BS = 512
HALF = 256
CHUNK = 128
STAT = CHUNK + 16
ROWS = CHUNK + STAT
LIMIT = 32 * 1024 * 1024

BF = jnp.bfloat16
F32 = jnp.float32

VM = pl.BlockSpec(memory_space=pltpu.VMEM)
SM = pl.BlockSpec(memory_space=pltpu.SMEM)
SQUARE = pltpu.VMEM((BS, BS), BF)


def call(kernel, shapes, specs, scratch=(), flops=0, nbytes=0):
    many = isinstance(shapes, tuple)
    return pl.pallas_call(
        kernel,
        out_shape=shapes,
        in_specs=specs,
        out_specs=(VM,) * len(shapes) if many else VM,
        scratch_shapes=list(scratch),
        compiler_params=pltpu.CompilerParams(vmem_limit_bytes=LIMIT),
        cost_estimate=pl.CostEstimate(flops=flops, bytes_accessed=nbytes, transcendentals=0),
    )


def array(*shape, dtype=BF):
    return jax.ShapeDtypeStruct(shape, dtype)


def place():
    group = lax.axis_index("group")
    return lax.rem(group, 2), lax.rem(lax.div(group, 2), 4), lax.div(group, 8)


def rows_at(core, chunk):
    return pl.ds(pl.multiple_of(core * HALF + chunk * CHUNK, CHUNK), CHUNK)


def mm(a, b):
    return jnp.dot(a.astype(BF), b.astype(BF), preferred_element_type=F32)


def grid_of(n):
    return lax.broadcasted_iota(jnp.int32, (n, n), 0), lax.broadcasted_iota(jnp.int32, (n, n), 1)


def first_kernel(grad, got, stat, out):
    core, _, _ = place()
    for y in range(4):
        mine = grad[y // 2, rows_at(core, y % 2), :].astype(F32)
        other = got[y // 2, (y % 2) * CHUNK : (y % 2 + 1) * CHUNK, :].astype(F32)
        out[y, 0:CHUNK, :] = (mine + other).astype(BF)
    row, col = grid_of(HALF)
    corner = stat[HALF:BS, HALF:BS]
    fold = jnp.where(row <= col, stat[0:HALF, 0:HALF], corner).astype(BF)
    diagonal = jnp.sum(jnp.where(row == col, corner, 0.0), axis=0, keepdims=True)
    diagonal = jnp.broadcast_to(diagonal, (16, HALF)).astype(BF)
    side = stat[0:HALF, HALF:BS].astype(BF)
    for y in range(4):
        lo = (y % 2) * CHUNK
        out[y, CHUNK : 2 * CHUNK, 0:HALF] = fold[lo : lo + CHUNK]
        out[y, CHUNK : 2 * CHUNK, HALF:BS] = side[lo : lo + CHUNK]
        out[y, 2 * CHUNK : ROWS, 0:HALF] = diagonal
        out[y, 2 * CHUNK : ROWS, HALF:BS] = diagonal


def unpack(packed, diagonal, stat):
    row, col = grid_of(HALF)
    fold = packed[:, 0:HALF].astype(F32)
    turned = fold.T
    stat[0:HALF, 0:HALF] = jnp.where(row <= col, fold, turned)
    stat[HALF:BS, HALF:BS] = jnp.where(row > col, fold, jnp.where(row < col, turned, diagonal))
    side = packed[:, HALF:BS].astype(F32)
    stat[0:HALF, HALF:BS] = side
    stat[HALF:BS, 0:HALF] = side.T


def second_kernel(owner, got, out):
    _, y, _ = place()
    total = got[0, 0:CHUNK, :].astype(F32)
    for source in range(1, 4):
        total += got[source, 0:CHUNK, :].astype(F32)
    out[0:CHUNK, :] = total.astype(BF)
    pair = owner[lax.axis_index("dp"), lax.div(y, 2)]
    out[CHUNK:ROWS, :] = got[lax.rem(pair, 4), CHUNK:ROWS, :]


def third_kernel(owner, mine, got, out):
    _, y, half = place()
    out[0:CHUNK, :] = (mine[0:CHUNK, :].astype(F32) + got[0:CHUNK, :].astype(F32)).astype(BF)
    here = lax.div(owner[lax.axis_index("dp"), lax.div(y, 2)], 4) == half

    @pl.when(here)
    def _():
        out[CHUNK:ROWS, :] = mine[CHUNK:ROWS, :]

    @pl.when(jnp.logical_not(here))
    def _():
        out[CHUNK:ROWS, :] = got[CHUNK:ROWS, :]


def gram_of(core, dense, oriented):
    @pl.when(core == 0)
    def _():
        oriented[...] = dense[...]

    @pl.when(core == 1)
    def _():
        oriented[...] = dense[...].astype(F32).T.astype(BF)

    value = oriented[...]
    return lax.dot_general(value, value, (((1,), (1,)), ((), ())), preferred_element_type=F32)


def newton(current):
    low = current.astype(BF)
    square = (1.0 / 16) * mm(low, low) - (10.0 / 16) * current
    slow = square.astype(BF)
    fourth = (50.0 / 16) * square + mm(slow, slow)
    return (625.0 / 256) * current + mm(fourth, low)


def root_kernel(mine, near, far, out, dense, oriented, packed, stat):
    core, y, _ = place()
    chunk = lax.rem(y, 2)
    dense[rows_at(core, chunk), :] = mine[0:CHUNK, :]
    dense[rows_at(core, 1 - chunk), :] = near[0:CHUNK, :]
    dense[rows_at(1 - core, chunk), :] = far[0]
    dense[rows_at(1 - core, 1 - chunk), :] = far[1]
    packed[rows_at(0, chunk), :] = mine[CHUNK : 2 * CHUNK, :]
    packed[rows_at(0, 1 - chunk), :] = near[CHUNK : 2 * CHUNK, :]
    unpack(packed, mine[2 * CHUNK : ROWS, 0:HALF].astype(F32)[0:1, :], stat)
    gram = gram_of(core, dense, oriented)
    row, col = grid_of(BS)
    shifted = BETA * stat[...] + (1.0 - BETA) * gram + jnp.where(row == col, DAMPING, 0.0)
    frob = jnp.sqrt(jnp.sum(shifted * shifted, keepdims=True))
    m0 = shifted * (1.0 / frob)
    m1 = newton(m0)
    m2 = newton(m1)
    n01 = (-1.25 / 4) * (m0 + m1) + (1.0 / 16) * mm(m0, m1)
    excess = 1.25 * n01 - (1.5625 / 4) * m2 - 0.25 * mm(n01, m2)
    scale = lax.rsqrt(jnp.sqrt(frob))

    @pl.when(core == 0)
    def _():
        block = dense[...]
        out[0:BS, :] = (scale * (1.953125 * block.astype(F32) + mm(excess, block))).astype(BF)
        out[BS : BS + 16, :] = jnp.zeros((16, BS), BF)

    @pl.when(core == 1)
    def _():
        out[0:BS, :] = excess.astype(BF)
        value = jnp.broadcast_to(scale, (16, BS))
        high = value.astype(BF).astype(F32)
        middle = (value - high).astype(BF).astype(F32)
        low = value - high - middle
        line = lax.broadcasted_iota(jnp.int32, (16, BS), 0)
        out[BS : BS + 16, :] = jnp.where(line == 0, high, jnp.where(line == 1, middle, low)).astype(BF)


def product_kernel(mine, other, dense, out, half_rows, left, right):
    core, _, _ = place()

    @pl.when(core == 0)
    def _():
        left[...] = mine[...]
        right[...] = other[...]

    @pl.when(core == 1)
    def _():
        left[...] = other[...]
        right[...] = mine[...]

    tail = right[BS : BS + 16, :].astype(F32)
    scale = tail[0:1, 0:1] + tail[1:2, 0:1] + tail[2:3, 0:1]
    low = left[0:BS, :]
    precond = scale * (1.953125 * low.astype(F32) + mm(low, right[0:BS, :]))
    value = dense[...].astype(F32)
    grad_sq = jnp.sum(value * value, keepdims=True)
    pre_sq = jnp.sum(precond * precond, keepdims=True)
    out[...] = (precond * jnp.sqrt(grad_sq / (pre_sq + 1e-06))).astype(BF)
    half_rows[...] = out[pl.ds(pl.multiple_of(core * HALF, HALF), HALF), :]


def stat_kernel(owner, dense, away, far, stat, out, chosen, oriented):
    core, y, half = place()
    column = lax.axis_index("dp")
    pair = half * 4 + y
    block = lax.div(y, 2)
    same = owner[column, block] == pair
    cross = owner[column, 1 - block] == pair

    @pl.when(same)
    def _():
        chosen[...] = dense[...]

    @pl.when(cross)
    def _():
        chunk = 1 - lax.rem(y, 2)
        chosen[rows_at(core, chunk), :] = away[0]
        chosen[rows_at(core, 1 - chunk), :] = away[1]
        chosen[rows_at(1 - core, chunk), :] = far[0]
        chosen[rows_at(1 - core, 1 - chunk), :] = far[1]

    active = jnp.logical_or(same, cross)

    @pl.when(active)
    def _():
        out[...] = BETA * stat[...] + (1.0 - BETA) * gram_of(core, chosen, oriented)

    @pl.when(jnp.logical_not(active))
    def _():
        out[...] = stat[...]


def last_kernel(mine, away, far, out):
    core, y, _ = place()
    block = lax.div(y, 2)
    out[block] = mine[...]
    out[1 - block, pl.ds(pl.multiple_of(core * HALF, HALF), HALF), :] = away[...]
    out[1 - block, pl.ds(pl.multiple_of((1 - core) * HALF, HALF), HALF), :] = far[...]


def body(grad, stats, owner):
    core = lax.axis_index("group") % 2
    along_y = [[h * 8 + 2 * k + c for k in range(4)] for h in range(2) for c in range(2)]

    def send(value, change):
        return lax.ppermute(value, "group", [(g, change(g)) for g in range(16)])

    def to_core(value):
        return send(value, lambda g: g ^ 1)

    def to_mate(value):
        return send(value, lambda g: g ^ 2)

    def to_mirror(value):
        return send(value, lambda g: g ^ 6)

    def to_half(value):
        return send(value, lambda g: g ^ 8)

    block = grad[0]
    stat = stats[0, 0]
    got = to_core(lax.dynamic_slice_in_dim(block, (1 - core) * HALF, HALF, 1))
    parts = call(first_kernel, array(4, ROWS, BS), [VM, VM, VM])(block, got, stat)
    parts = lax.all_to_all(parts, "group", 0, 0, tiled=True, axis_index_groups=along_y)
    mine = call(second_kernel, array(ROWS, BS), [SM, VM])(owner, parts)
    got = to_half(mine)
    mine = call(third_kernel, array(ROWS, BS), [SM, VM, VM])(owner, mine, got)
    near = to_mate(mine)
    both = jnp.stack([mine[:CHUNK], near[:CHUNK]])
    far = to_core(both)
    away = to_mirror(both)
    payload, dense = call(
        root_kernel,
        (array(BS + 16, BS), array(BS, BS)),
        [VM, VM, VM],
        [SQUARE, pltpu.VMEM((HALF, BS), BF), pltpu.VMEM((BS, BS), F32)],
        flops=10 * 2 * BS**3,
    )(mine, near, far)
    received = to_core(payload)
    away_far = to_core(away)
    tall = pltpu.VMEM((BS + 16, BS), BF)
    result, half_rows = call(
        product_kernel, (array(BS, BS), array(HALF, BS)), [VM, VM, VM], [tall, tall], flops=2 * BS**3
    )(payload, received, dense)
    mirror = to_mirror(half_rows)
    new_stat = call(
        stat_kernel,
        array(BS, BS, dtype=F32),
        [SM, VM, VM, VM, VM],
        [SQUARE, SQUARE],
        flops=2 * BS**3,
        nbytes=3 << 20,
    )(owner, dense, away, away_far, stat)
    update = call(last_kernel, array(2, BS, BS), [VM, VM, VM])(result, mirror, to_core(mirror))
    return (new_stat[None, None], update)


def solution(mesh):
    in_specs = (P("group", "dp", None, None), P("group", "dp", None, None), P())
    out_specs = (P("group", "dp", None, None), P("dp", None, None))
    return jax.shard_map(body, mesh=mesh, in_specs=in_specs, out_specs=out_specs, check_vma=False)
```

```python
import jax
import jax.numpy as jnp
from jax import lax
from jax.experimental import pallas as pl
from jax.experimental.pallas import tpu as pltpu
from jax.sharding import PartitionSpec as P

BETA = 0.9
DAMPING = 0.0001
BS = 512
HALF = 256
CHUNK = 128
STAT = CHUNK + 16
ROWS = CHUNK + STAT
LIMIT = 32 * 1024 * 1024

BF = jnp.bfloat16
F32 = jnp.float32

VM = pl.BlockSpec(memory_space=pltpu.VMEM)
SM = pl.BlockSpec(memory_space=pltpu.SMEM)
SQUARE = pltpu.VMEM((BS, BS), BF)


def call(kernel, shapes, specs, scratch=(), flops=0, nbytes=0):
    many = isinstance(shapes, tuple)
    return pl.pallas_call(
        kernel,
        out_shape=shapes,
        in_specs=specs,
        out_specs=(VM,) * len(shapes) if many else VM,
        scratch_shapes=list(scratch),
        compiler_params=pltpu.CompilerParams(vmem_limit_bytes=LIMIT),
        cost_estimate=pl.CostEstimate(flops=flops, bytes_accessed=nbytes, transcendentals=0),
    )


def array(*shape, dtype=BF):
    return jax.ShapeDtypeStruct(shape, dtype)


def place():
    group = lax.axis_index("group")
    return lax.rem(group, 2), lax.rem(lax.div(group, 2), 4), lax.div(group, 8)


def half_at(core):
    return pl.ds(pl.multiple_of(core * HALF, HALF), HALF)


def mm(a, b):
    return jnp.dot(a.astype(BF), b.astype(BF), preferred_element_type=F32)


def grid_of(n):
    return lax.broadcasted_iota(jnp.int32, (n, n), 0), lax.broadcasted_iota(jnp.int32, (n, n), 1)


def pack_kernel(stat, out):
    row, col = grid_of(HALF)
    corner = stat[HALF:BS, HALF:BS]
    fold = jnp.where(row <= col, stat[0:HALF, 0:HALF], corner).astype(BF)
    diagonal = jnp.sum(jnp.where(row == col, corner, 0.0), axis=0, keepdims=True)
    diagonal = jnp.broadcast_to(diagonal, (16, HALF)).astype(BF)
    side = stat[0:HALF, HALF:BS].astype(BF)
    for chunk in range(2):
        lo = chunk * CHUNK
        out[chunk, 0:CHUNK, 0:HALF] = fold[lo : lo + CHUNK]
        out[chunk, 0:CHUNK, HALF:BS] = side[lo : lo + CHUNK]
        out[chunk, CHUNK:STAT, 0:HALF] = diagonal
        out[chunk, CHUNK:STAT, HALF:BS] = diagonal


def first_kernel(keep, got, packed, out):
    for y in range(4):
        rows = slice((y % 2) * CHUNK, (y % 2 + 1) * CHUNK)
        out[y, 0:CHUNK, :] = (keep[y // 2, rows, :].astype(F32) + got[y // 2, rows, :].astype(F32)).astype(BF)
        out[y, CHUNK:ROWS, :] = packed[y % 2]


def unpack(packed, diagonal, stat):
    row, col = grid_of(HALF)
    fold = packed[:, 0:HALF].astype(F32)
    turned = fold.T
    stat[0:HALF, 0:HALF] = jnp.where(row <= col, fold, turned)
    stat[HALF:BS, HALF:BS] = jnp.where(row > col, fold, jnp.where(row < col, turned, diagonal))
    side = packed[:, HALF:BS].astype(F32)
    stat[0:HALF, HALF:BS] = side
    stat[HALF:BS, 0:HALF] = side.T


def second_kernel(owner, got, out):
    _, y, _ = place()
    total = got[0, 0:CHUNK, :].astype(F32)
    for source in range(1, 4):
        total += got[source, 0:CHUNK, :].astype(F32)
    out[0:CHUNK, :] = total.astype(BF)
    pair = owner[lax.axis_index("dp"), lax.div(y, 2)]
    out[CHUNK:ROWS, :] = got[lax.rem(pair, 4), CHUNK:ROWS, :]


def third_kernel(owner, got, out):
    _, y, _ = place()
    out[0:CHUNK, :] = (got[0, 0:CHUNK, :].astype(F32) + got[1, 0:CHUNK, :].astype(F32)).astype(BF)
    pair = owner[lax.axis_index("dp"), lax.div(y, 2)]
    out[CHUNK:ROWS, :] = got[lax.div(pair, 4), CHUNK:ROWS, :]


def gram_of(core, dense, oriented):
    @pl.when(core == 0)
    def _():
        oriented[...] = dense[...]

    @pl.when(core == 1)
    def _():
        oriented[...] = dense[...].astype(F32).T.astype(BF)

    value = oriented[...]
    return lax.dot_general(value, value, (((1,), (1,)), ((), ())), preferred_element_type=F32)


def newton(current):
    low = current.astype(BF)
    square = (1.0 / 16) * mm(low, low) - (10.0 / 16) * current
    slow = square.astype(BF)
    fourth = (50.0 / 16) * square + mm(slow, slow)
    return (625.0 / 256) * current + mm(fourth, low)


def root_kernel(pair, dense, out, oriented, packed, stat):
    core, _, _ = place()
    packed[0:CHUNK, :] = pair[0, CHUNK : 2 * CHUNK, :]
    packed[CHUNK:HALF, :] = pair[1, CHUNK : 2 * CHUNK, :]
    unpack(packed, pair[0, 2 * CHUNK : ROWS, 0:HALF].astype(F32)[0:1, :], stat)
    gram = gram_of(core, dense, oriented)
    row, col = grid_of(BS)
    shifted = BETA * stat[...] + (1.0 - BETA) * gram + jnp.where(row == col, DAMPING, 0.0)
    frob = jnp.sqrt(jnp.sum(shifted * shifted, keepdims=True))
    m0 = shifted * (1.0 / frob)
    m1 = newton(m0)
    m2 = newton(m1)
    n01 = (-1.25 / 4) * (m0 + m1) + (1.0 / 16) * mm(m0, m1)
    excess = 1.25 * n01 - (1.5625 / 4) * m2 - 0.25 * mm(n01, m2)
    scale = lax.rsqrt(jnp.sqrt(frob))

    @pl.when(core == 0)
    def _():
        block = dense[...]
        out[0:BS, :] = (scale * (1.953125 * block.astype(F32) + mm(excess, block))).astype(BF)
        out[BS : BS + 16, :] = jnp.zeros((16, BS), BF)

    @pl.when(core == 1)
    def _():
        out[0:BS, :] = excess.astype(BF)
        value = jnp.broadcast_to(scale, (16, BS))
        high = value.astype(BF).astype(F32)
        middle = (value - high).astype(BF).astype(F32)
        low = value - high - middle
        line = lax.broadcasted_iota(jnp.int32, (16, BS), 0)
        out[BS : BS + 16, :] = jnp.where(line == 0, high, jnp.where(line == 1, middle, low)).astype(BF)


def product_kernel(mine, other, dense, out, half_rows, left, right):
    core, _, _ = place()

    @pl.when(core == 0)
    def _():
        left[...] = mine[...]
        right[...] = other[...]

    @pl.when(core == 1)
    def _():
        left[...] = other[...]
        right[...] = mine[...]

    tail = right[BS : BS + 16, :].astype(F32)
    scale = tail[0:1, 0:1] + tail[1:2, 0:1] + tail[2:3, 0:1]
    low = left[0:BS, :]
    precond = scale * (1.953125 * low.astype(F32) + mm(low, right[0:BS, :]))
    value = dense[...].astype(F32)
    grad_sq = jnp.sum(value * value, keepdims=True)
    pre_sq = jnp.sum(precond * precond, keepdims=True)
    out[...] = (precond * jnp.sqrt(grad_sq / (pre_sq + 1e-06))).astype(BF)
    half_rows[...] = out[half_at(core), :]


def stat_kernel(owner, dense, away, far, stat, out, chosen, oriented):
    core, y, half = place()
    column = lax.axis_index("dp")
    pair = half * 4 + y
    block = lax.div(y, 2)
    same = owner[column, block] == pair
    cross = owner[column, 1 - block] == pair

    @pl.when(same)
    def _():
        chosen[...] = dense[...]

    @pl.when(cross)
    def _():
        chosen[half_at(core), :] = away[...]
        chosen[half_at(1 - core), :] = far[...]

    active = jnp.logical_or(same, cross)

    @pl.when(active)
    def _():
        out[...] = BETA * stat[...] + (1.0 - BETA) * gram_of(core, chosen, oriented)

    @pl.when(jnp.logical_not(active))
    def _():
        out[...] = stat[...]


def last_kernel(mine, other, out):
    _, y, _ = place()
    block = lax.div(y, 2)
    out[block] = mine[...]
    out[1 - block, 0:HALF, :] = other[0]
    out[1 - block, HALF:BS, :] = other[1]


def body(grad, stats, owner):
    core = lax.axis_index("group") % 2
    along_y = [[h * 8 + 2 * k + c for k in range(4)] for h in range(2) for c in range(2)]

    def send(value, bits):
        return lax.ppermute(value, "group", [(g, g ^ bits) for g in range(16)])

    def gather(value, bits):
        return lax.all_gather(value, "group", axis_index_groups=[[g, g ^ bits] for g in range(16) if g < g ^ bits])

    block = grad[0]
    stat = stats[0, 0]
    got = send(lax.dynamic_slice_in_dim(block, (1 - core) * HALF, HALF, 1), 1)
    keep = lax.dynamic_slice_in_dim(block, core * HALF, HALF, 1)
    packed = call(pack_kernel, array(2, STAT, BS), [VM], nbytes=3 << 19)(stat)
    parts = call(first_kernel, array(4, ROWS, BS), [VM, VM, VM])(keep, got, packed)
    parts = lax.all_to_all(parts, "group", 0, 0, tiled=True, axis_index_groups=along_y)
    partial = call(second_kernel, array(ROWS, BS), [SM, VM])(owner, parts)
    mine = call(third_kernel, array(ROWS, BS), [SM, VM])(owner, gather(partial, 8))
    pair = gather(mine, 2)
    rows = pair[:, :CHUNK].reshape(HALF, BS)
    away = send(rows, 6)
    dense = gather(rows, 1).reshape(BS, BS)
    payload = call(
        root_kernel,
        array(BS + 16, BS),
        [VM, VM],
        [SQUARE, pltpu.VMEM((HALF, BS), BF), pltpu.VMEM((BS, BS), F32)],
        flops=10 * 2 * BS**3,
    )(pair, dense)
    payload, away = lax.optimization_barrier((payload, away))
    received = send(payload, 1)
    away_far = send(away, 1)
    tall = pltpu.VMEM((BS + 16, BS), BF)
    result, half_rows = call(
        product_kernel, (array(BS, BS), array(HALF, BS)), [VM, VM, VM], [tall, tall], flops=2 * BS**3
    )(payload, received, dense)
    mirror = send(half_rows, 6)
    new_stat = call(
        stat_kernel,
        array(BS, BS, dtype=F32),
        [SM, VM, VM, VM, VM],
        [SQUARE, SQUARE],
        flops=2 * BS**3,
        nbytes=3 << 20,
    )(owner, dense, away, away_far, stat)
    update = call(last_kernel, array(2, BS, BS), [VM, VM])(result, gather(mirror, 1))
    return (new_stat[None, None], update)


def solution(mesh):
    in_specs = (P("group", "dp", None, None), P("group", "dp", None, None), P())
    out_specs = (P("group", "dp", None, None), P("dp", None, None))
    return jax.shard_map(body, mesh=mesh, in_specs=in_specs, out_specs=out_specs, check_vma=False)
```

```python
import jax
import jax.numpy as jnp
from jax import lax
from jax.experimental import pallas as pl
from jax.experimental.pallas import tpu as pltpu
from jax.sharding import PartitionSpec as P

BETA = 0.9
DAMPING = 0.0001
BS = 512
HALF = 256
CHUNK = 128
STAT = CHUNK + 16
ROWS = CHUNK + STAT
LIMIT = 32 * 1024 * 1024

BF = jnp.bfloat16
F32 = jnp.float32

VM = pl.BlockSpec(memory_space=pltpu.VMEM)
SM = pl.BlockSpec(memory_space=pltpu.SMEM)
SQUARE = pltpu.VMEM((BS, BS), BF)


def call(kernel, shapes, specs, scratch=(), flops=0, nbytes=0):
    many = isinstance(shapes, tuple)
    return pl.pallas_call(
        kernel,
        out_shape=shapes,
        in_specs=specs,
        out_specs=(VM,) * len(shapes) if many else VM,
        scratch_shapes=list(scratch),
        compiler_params=pltpu.CompilerParams(vmem_limit_bytes=LIMIT),
        cost_estimate=pl.CostEstimate(flops=flops, bytes_accessed=nbytes, transcendentals=0),
    )


def array(*shape, dtype=BF):
    return jax.ShapeDtypeStruct(shape, dtype)


def place():
    group = lax.axis_index("group")
    return lax.rem(group, 2), lax.rem(lax.div(group, 2), 4), lax.div(group, 8)


def half_at(core):
    return pl.ds(pl.multiple_of(core * HALF, HALF), HALF)


def mm(a, b):
    return jnp.dot(a.astype(BF), b.astype(BF), preferred_element_type=F32)


def grid_of(n):
    return lax.broadcasted_iota(jnp.int32, (n, n), 0), lax.broadcasted_iota(jnp.int32, (n, n), 1)


def pack_kernel(stat, out):
    row, col = grid_of(HALF)
    corner = stat[HALF:BS, HALF:BS]
    fold = jnp.where(row <= col, stat[0:HALF, 0:HALF], corner).astype(BF)
    diagonal = jnp.sum(jnp.where(row == col, corner, 0.0), axis=0, keepdims=True)
    diagonal = jnp.broadcast_to(diagonal, (16, HALF)).astype(BF)
    side = stat[0:HALF, HALF:BS].astype(BF)
    for y in range(4):
        lo = (y % 2) * CHUNK
        out[y, 0:CHUNK, 0:HALF] = fold[lo : lo + CHUNK]
        out[y, 0:CHUNK, HALF:BS] = side[lo : lo + CHUNK]
        out[y, CHUNK:STAT, 0:HALF] = diagonal
        out[y, CHUNK:STAT, HALF:BS] = diagonal


def first_kernel(keep, got, out):
    for y in range(4):
        rows = slice((y % 2) * CHUNK, (y % 2 + 1) * CHUNK)
        out[y] = (keep[y // 2, rows, :].astype(F32) + got[y // 2, rows, :].astype(F32)).astype(BF)


def unpack(packed, diagonal, stat):
    row, col = grid_of(HALF)
    fold = packed[:, 0:HALF].astype(F32)
    turned = fold.T
    stat[0:HALF, 0:HALF] = jnp.where(row <= col, fold, turned)
    stat[HALF:BS, HALF:BS] = jnp.where(row > col, fold, jnp.where(row < col, turned, diagonal))
    side = packed[:, HALF:BS].astype(F32)
    stat[0:HALF, HALF:BS] = side
    stat[HALF:BS, 0:HALF] = side.T


def choose_kernel(owner, got, out):
    _, y, _ = place()
    out[...] = got[lax.rem(owner[lax.axis_index("dp"), lax.div(y, 2)], 4)]


def second_kernel(got, out):
    total = got[0].astype(F32)
    for source in range(1, 4):
        total += got[source].astype(F32)
    out[...] = total.astype(BF)


def third_kernel(owner, sums, stat, other, out):
    _, y, half = place()
    out[0:CHUNK, :] = (sums[0].astype(F32) + sums[1].astype(F32)).astype(BF)
    here = lax.div(owner[lax.axis_index("dp"), lax.div(y, 2)], 4) == half

    @pl.when(here)
    def _():
        out[CHUNK:ROWS, :] = stat[...]

    @pl.when(jnp.logical_not(here))
    def _():
        out[CHUNK:ROWS, :] = other[...]


def gram_of(core, dense, oriented):
    @pl.when(core == 0)
    def _():
        oriented[...] = dense[...]

    @pl.when(core == 1)
    def _():
        oriented[...] = dense[...].astype(F32).T.astype(BF)

    value = oriented[...]
    return lax.dot_general(value, value, (((1,), (1,)), ((), ())), preferred_element_type=F32)


def newton(current):
    low = current.astype(BF)
    square = (1.0 / 16) * mm(low, low) - (10.0 / 16) * current
    slow = square.astype(BF)
    fourth = (50.0 / 16) * square + mm(slow, slow)
    return (625.0 / 256) * current + mm(fourth, low)


def root_kernel(pair, dense, out, oriented, packed, stat):
    core, _, _ = place()
    packed[0:CHUNK, :] = pair[0, CHUNK : 2 * CHUNK, :]
    packed[CHUNK:HALF, :] = pair[1, CHUNK : 2 * CHUNK, :]
    unpack(packed, pair[0, 2 * CHUNK : ROWS, 0:HALF].astype(F32)[0:1, :], stat)
    gram = gram_of(core, dense, oriented)
    row, col = grid_of(BS)
    shifted = BETA * stat[...] + (1.0 - BETA) * gram + jnp.where(row == col, DAMPING, 0.0)
    frob = jnp.sqrt(jnp.sum(shifted * shifted, keepdims=True))
    m0 = shifted * (1.0 / frob)
    m1 = newton(m0)
    m2 = newton(m1)
    n01 = (-1.25 / 4) * (m0 + m1) + (1.0 / 16) * mm(m0, m1)
    excess = 1.25 * n01 - (1.5625 / 4) * m2 - 0.25 * mm(n01, m2)
    scale = lax.rsqrt(jnp.sqrt(frob))

    @pl.when(core == 0)
    def _():
        block = dense[...]
        out[0:BS, :] = (scale * (1.953125 * block.astype(F32) + mm(excess, block))).astype(BF)
        out[BS : BS + 16, :] = jnp.zeros((16, BS), BF)

    @pl.when(core == 1)
    def _():
        out[0:BS, :] = excess.astype(BF)
        value = jnp.broadcast_to(scale, (16, BS))
        high = value.astype(BF).astype(F32)
        middle = (value - high).astype(BF).astype(F32)
        low = value - high - middle
        line = lax.broadcasted_iota(jnp.int32, (16, BS), 0)
        out[BS : BS + 16, :] = jnp.where(line == 0, high, jnp.where(line == 1, middle, low)).astype(BF)


def product_kernel(mine, other, dense, out, half_rows, left, right):
    core, _, _ = place()

    @pl.when(core == 0)
    def _():
        left[...] = mine[...]
        right[...] = other[...]

    @pl.when(core == 1)
    def _():
        left[...] = other[...]
        right[...] = mine[...]

    tail = right[BS : BS + 16, :].astype(F32)
    scale = tail[0:1, 0:1] + tail[1:2, 0:1] + tail[2:3, 0:1]
    low = left[0:BS, :]
    precond = scale * (1.953125 * low.astype(F32) + mm(low, right[0:BS, :]))
    value = dense[...].astype(F32)
    grad_sq = jnp.sum(value * value, keepdims=True)
    pre_sq = jnp.sum(precond * precond, keepdims=True)
    out[...] = (precond * jnp.sqrt(grad_sq / (pre_sq + 1e-06))).astype(BF)
    half_rows[...] = out[half_at(core), :]


def stat_kernel(owner, dense, away, far, stat, out, chosen, oriented):
    core, y, half = place()
    column = lax.axis_index("dp")
    pair = half * 4 + y
    block = lax.div(y, 2)
    same = owner[column, block] == pair
    cross = owner[column, 1 - block] == pair

    @pl.when(same)
    def _():
        chosen[...] = dense[...]

    @pl.when(cross)
    def _():
        chosen[half_at(core), :] = away[...]
        chosen[half_at(1 - core), :] = far[...]

    active = jnp.logical_or(same, cross)

    @pl.when(active)
    def _():
        out[...] = BETA * stat[...] + (1.0 - BETA) * gram_of(core, chosen, oriented)

    @pl.when(jnp.logical_not(active))
    def _():
        out[...] = stat[...]


def last_kernel(mine, other, out):
    _, y, _ = place()
    block = lax.div(y, 2)
    out[block] = mine[...]
    out[1 - block, 0:HALF, :] = other[0]
    out[1 - block, HALF:BS, :] = other[1]


def body(grad, stats, owner):
    core = lax.axis_index("group") % 2
    along_y = [[h * 8 + 2 * k + c for k in range(4)] for h in range(2) for c in range(2)]

    def send(value, bits):
        return lax.ppermute(value, "group", [(g, g ^ bits) for g in range(16)])

    def gather(value, bits):
        return lax.all_gather(value, "group", axis_index_groups=[[g, g ^ bits] for g in range(16) if g < g ^ bits])

    def exchange(value):
        return lax.all_to_all(value, "group", 0, 0, tiled=True, axis_index_groups=along_y)

    block = grad[0]
    stat = stats[0, 0]
    got = send(lax.dynamic_slice_in_dim(block, (1 - core) * HALF, HALF, 1), 1)
    keep = lax.dynamic_slice_in_dim(block, core * HALF, HALF, 1)
    packed = call(pack_kernel, array(4, STAT, BS), [VM], nbytes=3 << 19)(stat)
    chosen = call(choose_kernel, array(STAT, BS), [SM, VM])(owner, exchange(packed))
    parts = exchange(call(first_kernel, array(4, CHUNK, BS), [VM, VM])(keep, got))
    partial = call(second_kernel, array(CHUNK, BS), [VM])(parts)
    across = send(chosen, 8)
    sums = gather(partial, 8)
    mine = call(third_kernel, array(ROWS, BS), [SM, VM, VM, VM])(owner, sums, chosen, across)
    pair = gather(mine, 2)
    rows = pair[:, :CHUNK].reshape(HALF, BS)
    away = send(rows, 6)
    dense = gather(rows, 1).reshape(BS, BS)
    payload = call(
        root_kernel,
        array(BS + 16, BS),
        [VM, VM],
        [SQUARE, pltpu.VMEM((HALF, BS), BF), pltpu.VMEM((BS, BS), F32)],
        flops=10 * 2 * BS**3,
    )(pair, dense)
    payload, away = lax.optimization_barrier((payload, away))
    received = send(payload, 1)
    away_far = send(away, 1)
    tall = pltpu.VMEM((BS + 16, BS), BF)
    result, half_rows = call(
        product_kernel, (array(BS, BS), array(HALF, BS)), [VM, VM, VM], [tall, tall], flops=2 * BS**3
    )(payload, received, dense)
    mirror = send(half_rows, 6)
    new_stat = call(
        stat_kernel,
        array(BS, BS, dtype=F32),
        [SM, VM, VM, VM, VM],
        [SQUARE, SQUARE],
        flops=2 * BS**3,
        nbytes=3 << 20,
    )(owner, dense, away, away_far, stat)
    update = call(last_kernel, array(2, BS, BS), [VM, VM])(result, gather(mirror, 1))
    return (new_stat[None, None], update)


def solution(mesh):
    in_specs = (P("group", "dp", None, None), P("group", "dp", None, None), P())
    out_specs = (P("group", "dp", None, None), P("dp", None, None))
    return jax.shard_map(body, mesh=mesh, in_specs=in_specs, out_specs=out_specs, check_vma=False)
```

```python
import jax
import jax.numpy as jnp
from jax import lax
from jax.experimental import pallas as pl
from jax.experimental.pallas import tpu as pltpu
from jax.sharding import PartitionSpec as P

BETA = 0.9
DAMPING = 0.0001
BS = 512
HALF = 256
CHUNK = 128
STAT = CHUNK + 16
ROWS = CHUNK + STAT
LIMIT = 32 * 1024 * 1024

BF = jnp.bfloat16
F32 = jnp.float32

VM = pl.BlockSpec(memory_space=pltpu.VMEM)
HBM = pl.BlockSpec(memory_space=pl.ANY)
SQUARE = pltpu.VMEM((BS, BS), BF)


def call(kernel, shapes, specs, scratch=(), flops=0, nbytes=0, out_spec=VM, **more):
    many = isinstance(shapes, tuple)
    return pl.pallas_call(
        kernel,
        out_shape=shapes,
        in_specs=specs,
        out_specs=(out_spec,) * len(shapes) if many else out_spec,
        scratch_shapes=list(scratch),
        compiler_params=pltpu.CompilerParams(vmem_limit_bytes=LIMIT),
        cost_estimate=pl.CostEstimate(flops=flops, bytes_accessed=nbytes, transcendentals=0),
        **more,
    )


def array(*shape, dtype=BF):
    return jax.ShapeDtypeStruct(shape, dtype)


def place():
    group = lax.axis_index("group")
    return lax.rem(group, 2), lax.rem(lax.div(group, 2), 4), lax.div(group, 8)


def owner_of(owner, block):
    row = lax.broadcasted_iota(jnp.int32, owner.shape, 0) == lax.axis_index("dp")
    col = lax.broadcasted_iota(jnp.int32, owner.shape, 1) == block
    return jnp.sum(jnp.where(row & col, owner[...], 0))


def half_at(core):
    return pl.ds(pl.multiple_of(core * HALF, HALF), HALF)


def mm(a, b):
    return jnp.dot(a.astype(BF), b.astype(BF), preferred_element_type=F32)


def grid_of(n):
    return lax.broadcasted_iota(jnp.int32, (n, n), 0), lax.broadcasted_iota(jnp.int32, (n, n), 1)


def take(other):
    def kernel(grad, out, sems):
        core, _, _ = place()
        rows = half_at(1 - core if other else core)
        copies = [pltpu.make_async_copy(grad.at[b, rows, :], out.at[b], sems.at[b]) for b in range(2)]
        for copy in copies:
            copy.start()
        for copy in copies:
            copy.wait()

    return kernel


def pack_kernel(stat, out):
    row, col = grid_of(HALF)
    corner = stat[HALF:BS, HALF:BS]
    fold = jnp.where(row <= col, stat[0:HALF, 0:HALF], corner).astype(BF)
    diagonal = jnp.sum(jnp.where(row == col, corner, 0.0), axis=0, keepdims=True)
    diagonal = jnp.broadcast_to(diagonal, (16, HALF)).astype(BF)
    side = stat[0:HALF, HALF:BS].astype(BF)
    for chunk in range(2):
        lo = chunk * CHUNK
        out[chunk, 0:CHUNK, 0:HALF] = fold[lo : lo + CHUNK]
        out[chunk, 0:CHUNK, HALF:BS] = side[lo : lo + CHUNK]
        out[chunk, CHUNK:STAT, 0:HALF] = diagonal
        out[chunk, CHUNK:STAT, HALF:BS] = diagonal


def first_kernel(keep, got, packed, owner, out):
    del owner
    for y in range(4):
        rows = slice((y % 2) * CHUNK, (y % 2 + 1) * CHUNK)
        out[y, 0:CHUNK, :] = (keep[y // 2, rows, :].astype(F32) + got[y // 2, rows, :].astype(F32)).astype(BF)
        out[y, CHUNK:ROWS, :] = packed[y % 2]


def unpack(packed, diagonal, stat):
    row, col = grid_of(HALF)
    fold = packed[:, 0:HALF].astype(F32)
    turned = fold.T
    stat[0:HALF, 0:HALF] = jnp.where(row <= col, fold, turned)
    stat[HALF:BS, HALF:BS] = jnp.where(row > col, fold, jnp.where(row < col, turned, diagonal))
    side = packed[:, HALF:BS].astype(F32)
    stat[0:HALF, HALF:BS] = side
    stat[HALF:BS, 0:HALF] = side.T


def second_kernel(owner, got, out):
    _, y, _ = place()
    total = got[0, 0:CHUNK, :].astype(F32)
    for source in range(1, 4):
        total += got[source, 0:CHUNK, :].astype(F32)
    out[0:CHUNK, :] = total.astype(BF)
    pair = owner_of(owner, lax.div(y, 2))
    out[CHUNK:ROWS, :] = got[lax.rem(pair, 4), CHUNK:ROWS, :]


def third_kernel(owner, got, out):
    _, y, _ = place()
    out[0:CHUNK, :] = (got[0, 0:CHUNK, :].astype(F32) + got[1, 0:CHUNK, :].astype(F32)).astype(BF)
    pair = owner_of(owner, lax.div(y, 2))
    out[CHUNK:ROWS, :] = got[lax.div(pair, 4), CHUNK:ROWS, :]


def gram_of(core, dense, oriented):
    @pl.when(core == 0)
    def _():
        oriented[...] = dense[...]

    @pl.when(core == 1)
    def _():
        oriented[...] = dense[...].astype(F32).T.astype(BF)

    value = oriented[...]
    return lax.dot_general(value, value, (((1,), (1,)), ((), ())), preferred_element_type=F32)


def newton(current):
    low = current.astype(BF)
    square = (1.0 / 16) * mm(low, low) - (10.0 / 16) * current
    slow = square.astype(BF)
    fourth = (50.0 / 16) * square + mm(slow, slow)
    return (625.0 / 256) * current + mm(fourth, low)


def root_kernel(pair, dense, out, oriented, packed, stat):
    core, _, _ = place()
    packed[0:CHUNK, :] = pair[0, CHUNK : 2 * CHUNK, :]
    packed[CHUNK:HALF, :] = pair[1, CHUNK : 2 * CHUNK, :]
    unpack(packed, pair[0, 2 * CHUNK : ROWS, 0:HALF].astype(F32)[0:1, :], stat)
    gram = gram_of(core, dense, oriented)
    row, col = grid_of(BS)
    shifted = BETA * stat[...] + (1.0 - BETA) * gram + jnp.where(row == col, DAMPING, 0.0)
    frob = jnp.sqrt(jnp.sum(shifted * shifted, keepdims=True))
    m0 = shifted * (1.0 / frob)
    m1 = newton(m0)
    m2 = newton(m1)
    n01 = (-1.25 / 4) * (m0 + m1) + (1.0 / 16) * mm(m0, m1)
    excess = 1.25 * n01 - (1.5625 / 4) * m2 - 0.25 * mm(n01, m2)
    scale = lax.rsqrt(jnp.sqrt(frob))

    @pl.when(core == 0)
    def _():
        block = dense[...]
        out[0:BS, :] = (scale * (1.953125 * block.astype(F32) + mm(excess, block))).astype(BF)
        out[BS : BS + 16, :] = jnp.zeros((16, BS), BF)

    @pl.when(core == 1)
    def _():
        out[0:BS, :] = excess.astype(BF)
        value = jnp.broadcast_to(scale, (16, BS))
        high = value.astype(BF).astype(F32)
        middle = (value - high).astype(BF).astype(F32)
        low = value - high - middle
        line = lax.broadcasted_iota(jnp.int32, (16, BS), 0)
        out[BS : BS + 16, :] = jnp.where(line == 0, high, jnp.where(line == 1, middle, low)).astype(BF)


def product_kernel(mine, other, dense, out, half_rows, left, right):
    core, _, _ = place()

    @pl.when(core == 0)
    def _():
        left[...] = mine[...]
        right[...] = other[...]

    @pl.when(core == 1)
    def _():
        left[...] = other[...]
        right[...] = mine[...]

    tail = right[BS : BS + 16, :].astype(F32)
    scale = tail[0:1, 0:1] + tail[1:2, 0:1] + tail[2:3, 0:1]
    low = left[0:BS, :]
    precond = scale * (1.953125 * low.astype(F32) + mm(low, right[0:BS, :]))
    value = dense[...].astype(F32)
    grad_sq = jnp.sum(value * value, keepdims=True)
    pre_sq = jnp.sum(precond * precond, keepdims=True)
    out[...] = (precond * jnp.sqrt(grad_sq / (pre_sq + 1e-06))).astype(BF)
    half_rows[...] = out[half_at(core), :]


def stat_kernel(owner, dense, away, far, stat, out, chosen, oriented):
    core, y, half = place()
    pair = half * 4 + y
    block = lax.div(y, 2)
    same = owner_of(owner, block) == pair
    cross = owner_of(owner, 1 - block) == pair

    @pl.when(same)
    def _():
        chosen[...] = dense[...]

    @pl.when(cross)
    def _():
        chosen[half_at(core), :] = away[...]
        chosen[half_at(1 - core), :] = far[...]

    active = jnp.logical_or(same, cross)

    @pl.when(active)
    def _():
        out[...] = BETA * stat[...] + (1.0 - BETA) * gram_of(core, chosen, oriented)

    @pl.when(jnp.logical_not(active))
    def _():
        out[...] = stat[...]


def own_kernel(mine, out, sem):
    _, y, _ = place()
    copy = pltpu.make_async_copy(mine, out.at[lax.div(y, 2)], sem)
    copy.start()
    copy.wait()


def last_kernel(other, begun, out, sem):
    del begun
    _, y, _ = place()
    copy = pltpu.make_async_copy(other, out.at[1 - lax.div(y, 2)], sem)
    copy.start()
    copy.wait()


def body(grad, stats, owner):
    along_y = [[h * 8 + 2 * k + c for k in range(4)] for h in range(2) for c in range(2)]

    def send(value, bits):
        return lax.ppermute(value, "group", [(g, g ^ bits) for g in range(16)])

    def gather(value, bits):
        return lax.all_gather(value, "group", axis_index_groups=[[g, g ^ bits] for g in range(16) if g < g ^ bits])

    block = grad[0]
    stat = stats[0, 0]
    pieces = [call(take(other), array(2, HALF, BS), [HBM], [pltpu.SemaphoreType.DMA((2,))]) for other in (True, False)]
    got = send(pieces[0](block), 1)
    keep = pieces[1](block)
    packed = call(pack_kernel, array(2, STAT, BS), [VM], nbytes=3 << 19)(stat)
    parts = call(first_kernel, array(4, ROWS, BS), [VM, VM, VM, VM])(keep, got, packed, owner)
    parts = lax.all_to_all(parts, "group", 0, 0, tiled=True, axis_index_groups=along_y)
    partial = call(second_kernel, array(ROWS, BS), [VM, VM])(owner, parts)
    mine = call(third_kernel, array(ROWS, BS), [VM, VM])(owner, gather(partial, 8))
    pair = gather(mine, 2)
    rows = pair[:, :CHUNK].reshape(HALF, BS)
    away = send(rows, 6)
    dense = gather(rows, 1).reshape(BS, BS)
    payload = call(
        root_kernel,
        array(BS + 16, BS),
        [VM, VM],
        [SQUARE, pltpu.VMEM((HALF, BS), BF), pltpu.VMEM((BS, BS), F32)],
        flops=10 * 2 * BS**3,
    )(pair, dense)
    payload, away = lax.optimization_barrier((payload, away))
    received = send(payload, 1)
    away_far = send(away, 1)
    tall = pltpu.VMEM((BS + 16, BS), BF)
    result, half_rows = call(
        product_kernel, (array(BS, BS), array(HALF, BS)), [VM, VM, VM], [tall, tall], flops=2 * BS**3
    )(payload, received, dense)
    mirror = send(half_rows, 6)
    new_stat = call(
        stat_kernel,
        array(BS, BS, dtype=F32),
        [VM, VM, VM, VM, VM],
        [SQUARE, SQUARE],
        flops=2 * BS**3,
        nbytes=3 << 20,
    )(owner, dense, away, away_far, stat)
    sem = [pltpu.SemaphoreType.DMA]
    begun = call(own_kernel, array(2, BS, BS), [VM], sem, out_spec=HBM)(result)
    other = gather(mirror, 1).reshape(BS, BS)
    update = call(last_kernel, array(2, BS, BS), [VM, HBM], sem, out_spec=HBM, input_output_aliases={1: 0})(other, begun)
    return (new_stat[None, None], update)


def solution(mesh):
    in_specs = (P("group", "dp", None, None), P("group", "dp", None, None), P())
    out_specs = (P("group", "dp", None, None), P("dp", None, None))
    return jax.shard_map(body, mesh=mesh, in_specs=in_specs, out_specs=out_specs, check_vma=False)
```

```python
import jax
import jax.numpy as jnp
from jax import lax
from jax.experimental import pallas as pl
from jax.experimental.pallas import tpu as pltpu
from jax.sharding import PartitionSpec as P

BETA = 0.9
DAMPING = 0.0001
BS = 512
HALF = 256
CHUNK = 64
TILE = 16
STAT = CHUNK + TILE
PART = 2 * CHUNK + STAT
ROWS = 4 * CHUNK + TILE
LIMIT = 40 * 1024 * 1024

BF = jnp.bfloat16
F32 = jnp.float32

VM = pl.BlockSpec(memory_space=pltpu.VMEM)
HBM = pl.BlockSpec(memory_space=pl.ANY)
BLOCKS = range(2)


def call(kernel, shapes, specs, scratch=(), flops=0, nbytes=0, out_spec=VM, **more):
    many = isinstance(shapes, tuple)
    return pl.pallas_call(
        kernel,
        out_shape=shapes,
        in_specs=specs,
        out_specs=(out_spec,) * len(shapes) if many else out_spec,
        scratch_shapes=list(scratch),
        compiler_params=pltpu.CompilerParams(vmem_limit_bytes=LIMIT),
        cost_estimate=pl.CostEstimate(flops=flops, bytes_accessed=nbytes, transcendentals=0),
        **more,
    )


def array(*shape, dtype=BF):
    return jax.ShapeDtypeStruct(shape, dtype)


def place():
    group = lax.axis_index("group")
    return lax.rem(group, 2), lax.rem(lax.div(group, 2), 4), lax.div(group, 8)


def owner_of(owner, block):
    row = lax.broadcasted_iota(jnp.int32, owner.shape, 0) == lax.axis_index("dp")
    col = lax.broadcasted_iota(jnp.int32, owner.shape, 1) == block
    return jnp.sum(jnp.where(row & col, owner[...], 0))


def half_at(core):
    return pl.ds(pl.multiple_of(core * HALF, HALF), HALF)


def mm(a, b):
    return jnp.dot(a.astype(BF), b.astype(BF), preferred_element_type=F32)


def grid_of(n):
    return lax.broadcasted_iota(jnp.int32, (n, n), 0), lax.broadcasted_iota(jnp.int32, (n, n), 1)


def take(other):
    def kernel(grad, out, sems):
        core, _, _ = place()
        rows = half_at(1 - core if other else core)
        copies = [pltpu.make_async_copy(grad.at[b, rows, :], out.at[b], sems.at[b]) for b in range(2)]
        for copy in copies:
            copy.start()
        for copy in copies:
            copy.wait()

    return kernel


def pack_kernel(stat, out):
    row, col = grid_of(HALF)
    corner = stat[HALF:BS, HALF:BS]
    fold = jnp.where(row <= col, stat[0:HALF, 0:HALF], corner).astype(BF)
    diagonal = jnp.sum(jnp.where(row == col, corner, 0.0), axis=0, keepdims=True)
    diagonal = jnp.broadcast_to(diagonal, (TILE, HALF)).astype(BF)
    side = stat[0:HALF, HALF:BS].astype(BF)
    for y in range(4):
        lo = y * CHUNK
        out[y, 0:CHUNK, 0:HALF] = fold[lo : lo + CHUNK]
        out[y, 0:CHUNK, HALF:BS] = side[lo : lo + CHUNK]
        out[y, CHUNK:STAT, 0:HALF] = diagonal
        out[y, CHUNK:STAT, HALF:BS] = diagonal


def first_kernel(keep, got, packed, owner, out):
    del owner
    for y in range(4):
        rows = slice(y * CHUNK, (y + 1) * CHUNK)
        for b in BLOCKS:
            total = (keep[b, rows, :].astype(F32) + got[b, rows, :].astype(F32)).astype(BF)
            out[y, b * CHUNK : (b + 1) * CHUNK, :] = total
        out[y, 2 * CHUNK : PART, :] = packed[y]


def join(first, second):
    row = lax.broadcasted_iota(jnp.int32, (TILE, BS), 0)
    return jnp.where(row < TILE // 2, first.astype(F32), second.astype(F32)).astype(BF)


def second_kernel(owner, got, out):
    total = got[0, 0 : 2 * CHUNK, :].astype(F32)
    for source in range(1, 4):
        total += got[source, 0 : 2 * CHUNK, :].astype(F32)
    out[0 : 2 * CHUNK, :] = total.astype(BF)
    source = [lax.rem(owner_of(owner, b), 4) for b in BLOCKS]
    for b in BLOCKS:
        out[(2 + b) * CHUNK : (3 + b) * CHUNK, :] = got[source[b], 2 * CHUNK : 3 * CHUNK, :]
    out[4 * CHUNK : ROWS, :] = join(*(got[source[b], 3 * CHUNK : PART, :] for b in BLOCKS))


def third_kernel(owner, got, out):
    total = (got[0, 0 : 2 * CHUNK, :].astype(F32) + got[1, 0 : 2 * CHUNK, :].astype(F32)).astype(BF)
    half = [lax.div(owner_of(owner, b), 4) for b in BLOCKS]
    stats = [got[half[b], (2 + b) * CHUNK : (3 + b) * CHUNK, :] for b in BLOCKS]
    diagonals = join(*(got[half[b], 4 * CHUNK : ROWS, :] for b in BLOCKS))
    for y in range(4):
        out[y, 0 : 2 * CHUNK, :] = total
        for b in BLOCKS:
            out[y, (2 + b) * CHUNK : (3 + b) * CHUNK, :] = stats[b]
        out[y, 4 * CHUNK : ROWS, :] = diagonals


def unpack_kernel(got, out):
    row, col = grid_of(HALF)
    damping = jnp.where(row == col, DAMPING, 0.0)
    tile = got[0, 4 * CHUNK : ROWS, 0:HALF].astype(F32)
    for b in BLOCKS:
        rows = slice((2 + b) * CHUNK, (3 + b) * CHUNK)
        packed = BETA * jnp.concatenate([got[y, rows, :] for y in range(4)], axis=0).astype(F32)
        fold = packed[:, 0:HALF]
        turned = fold.T
        at = b * (TILE // 2)
        diagonal = BETA * tile[at : at + 1, :]
        out[b, 0:HALF, 0:HALF] = jnp.where(row <= col, fold, turned) + damping
        out[b, HALF:BS, HALF:BS] = jnp.where(row > col, fold, jnp.where(row < col, turned, diagonal)) + damping
        side = packed[:, HALF:BS]
        out[b, 0:HALF, HALF:BS] = side
        out[b, HALF:BS, 0:HALF] = side.T


def gram_of(core, dense, oriented):
    @pl.when(core == 0)
    def _():
        oriented[...] = dense[...]

    @pl.when(core == 1)
    def _():
        oriented[...] = dense[...].astype(F32).T.astype(BF)

    value = oriented[...]
    return lax.dot_general(value, value, (((1,), (1,)), ((), ())), preferred_element_type=F32)


def newton(currents):
    lows = [m.astype(BF) for m in currents]
    squares = [(1.0 / 16) * mm(low, low) - (10.0 / 16) * m for low, m in zip(lows, currents)]
    slows = [square.astype(BF) for square in squares]
    fourths = [(50.0 / 16) * square + mm(slow, slow) for square, slow in zip(squares, slows)]
    return [(625.0 / 256) * m + mm(fourth, low) for fourth, low, m in zip(fourths, lows, currents)]


def root_kernel(got, far, stat, out, dense, oriented):
    core, _, _ = place()
    for b in BLOCKS:
        rows = slice(b * CHUNK, (b + 1) * CHUNK)
        for y in range(4):
            for where, source in ((core, got), (1 - core, far)):
                at = pl.multiple_of(where * HALF + y * CHUNK, CHUNK)
                dense[b, pl.ds(at, CHUNK), :] = source[y, rows, :]
    shifted = [stat[b] + (1.0 - BETA) * gram_of(core, dense.at[b], oriented.at[b]) for b in BLOCKS]
    frobs = [jnp.sqrt(jnp.sum(m * m, keepdims=True)) for m in shifted]
    m0 = [m * (1.0 / frob) for m, frob in zip(shifted, frobs)]
    m1 = newton(m0)
    m2 = newton(m1)
    n01 = [(-1.25 / 4) * (p + q) + (1.0 / 16) * mm(p, q) for p, q in zip(m0, m1)]
    excess = [1.25 * n - (1.5625 / 4) * m - 0.25 * mm(n, m) for n, m in zip(n01, m2)]
    scales = [lax.rsqrt(jnp.sqrt(frob)) for frob in frobs]

    @pl.when(core == 0)
    def _():
        for b in BLOCKS:
            block = dense[b]
            value = scales[b] * (1.953125 * block.astype(F32) + mm(excess[b], block))
            out[b * BS : (b + 1) * BS, :] = value.astype(BF)
        out[2 * BS : 2 * BS + TILE, :] = jnp.zeros((TILE, BS), BF)

    @pl.when(core == 1)
    def _():
        line = lax.broadcasted_iota(jnp.int32, (TILE, BS), 0)
        tail = jnp.zeros((TILE, BS), F32)
        for b in BLOCKS:
            out[b * BS : (b + 1) * BS, :] = excess[b].astype(BF)
            value = jnp.broadcast_to(scales[b], (TILE, BS))
            for term in range(3):
                high = value.astype(BF).astype(F32)
                tail = jnp.where(line == b * (TILE // 2) + term, high, tail)
                value = value - high
        out[2 * BS : 2 * BS + TILE, :] = tail.astype(BF)


def stat_kernel(owner, dense, stat, out, oriented):
    core, y, half = place()
    pair = half * 4 + y
    owned = [owner_of(owner, b) == pair for b in BLOCKS]
    for b in BLOCKS:

        @pl.when(owned[b])
        def _():
            out[...] = BETA * stat[...] + (1.0 - BETA) * gram_of(core, dense.at[b], oriented)

    @pl.when(jnp.logical_not(jnp.logical_or(*owned)))
    def _():
        out[...] = stat[...]


def product_kernel(mine, other, dense, out, done, sems):
    core, _, _ = place()

    def products(left, right):
        tail = right[2 * BS : 2 * BS + TILE, :].astype(F32)
        for b in BLOCKS:
            at = b * (TILE // 2)
            scale = tail[at : at + 1, 0:1] + tail[at + 1 : at + 2, 0:1] + tail[at + 2 : at + 3, 0:1]
            rows = slice(b * BS, (b + 1) * BS)
            low = left[rows, :]
            precond = scale * (1.953125 * low.astype(F32) + mm(low, right[rows, :]))
            value = dense[b].astype(F32)
            grad_sq = jnp.sum(value * value, keepdims=True)
            pre_sq = jnp.sum(precond * precond, keepdims=True)
            done[b] = (precond * jnp.sqrt(grad_sq / (pre_sq + 1e-06))).astype(BF)
            pltpu.make_async_copy(done.at[b], out.at[b], sems.at[b]).start()

    @pl.when(core == 0)
    def _():
        products(mine, other)

    @pl.when(core == 1)
    def _():
        products(other, mine)

    for b in BLOCKS:
        pltpu.make_async_copy(done.at[b], out.at[b], sems.at[b]).wait()


def body(grad, stats, owner):
    along_y = [[h * 8 + 2 * k + c for k in range(4)] for h in range(2) for c in range(2)]

    def send(value, bits):
        return lax.ppermute(value, "group", [(g, g ^ bits) for g in range(16)])

    def gather(value, bits):
        return lax.all_gather(value, "group", axis_index_groups=[[g, g ^ bits] for g in range(16) if g < g ^ bits])

    def exchange(value):
        return lax.all_to_all(value, "group", 0, 0, tiled=True, axis_index_groups=along_y)

    block = grad[0]
    stat = stats[0, 0]
    pieces = [call(take(other), array(2, HALF, BS), [HBM], [pltpu.SemaphoreType.DMA((2,))]) for other in (True, False)]
    got = send(pieces[0](block), 1)
    keep = pieces[1](block)
    packed = call(pack_kernel, array(4, STAT, BS), [VM], nbytes=3 << 19)(stat)
    parts = exchange(call(first_kernel, array(4, PART, BS), [VM, VM, VM, VM])(keep, got, packed, owner))
    partial = call(second_kernel, array(ROWS, BS), [VM, VM])(owner, parts)
    parts = exchange(call(third_kernel, array(4, ROWS, BS), [VM, VM])(owner, gather(partial, 8)))
    far = send(parts[:, : 2 * CHUNK], 1)
    shifted = call(unpack_kernel, array(2, BS, BS, dtype=F32), [VM], nbytes=5 << 19)(parts)
    pair = pltpu.VMEM((2, BS, BS), BF)
    payload, dense = call(
        root_kernel, (array(2 * BS + TILE, BS), array(2, BS, BS)), [VM, VM, VM], [pair], flops=20 * 2 * BS**3
    )(parts, far, shifted)
    received = send(payload, 1)
    new_stat = call(
        stat_kernel, array(BS, BS, dtype=F32), [VM, VM, VM], [pltpu.VMEM((BS, BS), BF)], flops=2 * BS**3, nbytes=3 << 20
    )(owner, dense, stat)
    update = call(
        product_kernel,
        array(2, BS, BS),
        [VM, VM, VM],
        [pair, pltpu.SemaphoreType.DMA((2,))],
        flops=4 * BS**3,
        out_spec=HBM,
    )(payload, received, dense)
    return (new_stat[None, None], update)


def solution(mesh):
    in_specs = (P("group", "dp", None, None), P("group", "dp", None, None), P())
    out_specs = (P("group", "dp", None, None), P("dp", None, None))
    return jax.shard_map(body, mesh=mesh, in_specs=in_specs, out_specs=out_specs, check_vma=False)
```

```python
import jax
import jax.numpy as jnp
from jax import lax
from jax.experimental import pallas as pl
from jax.experimental.pallas import tpu as pltpu
from jax.sharding import PartitionSpec as P

BETA = 0.9
DAMPING = 0.0001
BS = 512
HALF = 256
CHUNK = 64
TILE = 8
STAT = CHUNK + TILE
PART = 2 * CHUNK + STAT
ROWS = 4 * CHUNK + TILE
TAIL = 16
LIMIT = 40 * 1024 * 1024

BF = jnp.bfloat16
F32 = jnp.float32

VM = pl.BlockSpec(memory_space=pltpu.VMEM)
HBM = pl.BlockSpec(memory_space=pl.ANY)
BLOCKS = range(2)


def call(kernel, shapes, specs, scratch=(), flops=0, nbytes=0, out_spec=VM, **more):
    many = isinstance(shapes, tuple)
    return pl.pallas_call(
        kernel,
        out_shape=shapes,
        in_specs=specs,
        out_specs=(out_spec,) * len(shapes) if many else out_spec,
        scratch_shapes=list(scratch),
        compiler_params=pltpu.CompilerParams(vmem_limit_bytes=LIMIT),
        cost_estimate=pl.CostEstimate(flops=flops, bytes_accessed=nbytes, transcendentals=0),
        **more,
    )


def array(*shape, dtype=BF):
    return jax.ShapeDtypeStruct(shape, dtype)


def place():
    group = lax.axis_index("group")
    return lax.rem(group, 2), lax.rem(lax.div(group, 2), 4), lax.div(group, 8)


def owner_of(owner, block):
    row = lax.broadcasted_iota(jnp.int32, owner.shape, 0) == lax.axis_index("dp")
    col = lax.broadcasted_iota(jnp.int32, owner.shape, 1) == block
    return jnp.sum(jnp.where(row & col, owner[...], 0))


def half_at(core):
    return pl.ds(pl.multiple_of(core * HALF, HALF), HALF)


def mm(a, b):
    return jnp.dot(a.astype(BF), b.astype(BF), preferred_element_type=F32)


def grid_of(n):
    return lax.broadcasted_iota(jnp.int32, (n, n), 0), lax.broadcasted_iota(jnp.int32, (n, n), 1)


def take(other):
    def kernel(grad, out, sems):
        core, _, _ = place()
        rows = half_at(1 - core if other else core)
        copies = [pltpu.make_async_copy(grad.at[b, rows, :], out.at[b], sems.at[b]) for b in range(2)]
        for copy in copies:
            copy.start()
        for copy in copies:
            copy.wait()

    return kernel


def pack_kernel(stat, out):
    row, col = grid_of(HALF)
    corner = stat[HALF:BS, HALF:BS]
    fold = jnp.where(row <= col, stat[0:HALF, 0:HALF], corner).astype(BF)
    diagonal = jnp.sum(jnp.where(row == col, corner, 0.0), axis=0, keepdims=True)
    diagonal = jnp.broadcast_to(diagonal, (TILE, HALF)).astype(BF)
    side = stat[0:HALF, HALF:BS].astype(BF)
    for y in range(4):
        lo = y * CHUNK
        out[y, 0:CHUNK, 0:HALF] = fold[lo : lo + CHUNK]
        out[y, 0:CHUNK, HALF:BS] = side[lo : lo + CHUNK]
        out[y, CHUNK:STAT, 0:HALF] = diagonal
        out[y, CHUNK:STAT, HALF:BS] = diagonal


def first_kernel(keep, got, packed, owner, out):
    del owner
    for y in range(4):
        rows = slice(y * CHUNK, (y + 1) * CHUNK)
        for b in BLOCKS:
            total = (keep[b, rows, :].astype(F32) + got[b, rows, :].astype(F32)).astype(BF)
            out[y, b * CHUNK : (b + 1) * CHUNK, :] = total
        out[y, 2 * CHUNK : PART, :] = packed[y]


def join(first, second):
    row = lax.broadcasted_iota(jnp.int32, (TILE, BS), 0)
    return jnp.where(row < TILE // 2, first.astype(F32), second.astype(F32)).astype(BF)


def second_kernel(owner, got, out):
    total = got[0, 0 : 2 * CHUNK, :].astype(F32)
    for source in range(1, 4):
        total += got[source, 0 : 2 * CHUNK, :].astype(F32)
    out[0 : 2 * CHUNK, :] = total.astype(BF)
    source = [lax.rem(owner_of(owner, b), 4) for b in BLOCKS]
    for b in BLOCKS:
        out[(2 + b) * CHUNK : (3 + b) * CHUNK, :] = got[source[b], 2 * CHUNK : 3 * CHUNK, :]
    out[4 * CHUNK : ROWS, :] = join(*(got[source[b], 3 * CHUNK : PART, :] for b in BLOCKS))


def third_kernel(owner, got, out):
    total = (got[0, 0 : 2 * CHUNK, :].astype(F32) + got[1, 0 : 2 * CHUNK, :].astype(F32)).astype(BF)
    half = [lax.div(owner_of(owner, b), 4) for b in BLOCKS]
    stats = [got[half[b], (2 + b) * CHUNK : (3 + b) * CHUNK, :] for b in BLOCKS]
    diagonals = join(*(got[half[b], 4 * CHUNK : ROWS, :] for b in BLOCKS))
    for y in range(4):
        out[y, 0 : 2 * CHUNK, :] = total
        for b in BLOCKS:
            out[y, (2 + b) * CHUNK : (3 + b) * CHUNK, :] = stats[b]
        out[y, 4 * CHUNK : ROWS, :] = diagonals


def unpack_kernel(got, out):
    row, col = grid_of(HALF)
    damping = jnp.where(row == col, DAMPING, 0.0)
    tile = got[0, 4 * CHUNK : ROWS, 0:HALF].astype(F32)
    for b in BLOCKS:
        rows = slice((2 + b) * CHUNK, (3 + b) * CHUNK)
        packed = BETA * jnp.concatenate([got[y, rows, :] for y in range(4)], axis=0).astype(F32)
        fold = packed[:, 0:HALF]
        turned = fold.T
        at = b * (TILE // 2)
        diagonal = BETA * tile[at : at + 1, :]
        out[b, 0] = jnp.where(row <= col, fold, turned) + damping
        out[b, 1] = packed[:, HALF:BS]
        out[b, 2] = jnp.where(row > col, fold, jnp.where(row < col, turned, diagonal)) + damping


def whole(corners):
    first, side, last = (corner.astype(BF) for corner in corners)
    top = jnp.concatenate([first, side], axis=1)
    return jnp.concatenate([top, jnp.concatenate([side.T, last], axis=1)], axis=0)


def corners_of(left, right, contract):
    numbers = (((1,), (contract,)), ((), ()))
    top = lax.dot_general(left[0:HALF], right, numbers, preferred_element_type=F32)
    tail = right[:, HALF:BS] if contract == 0 else right[HALF:BS]
    last = lax.dot_general(left[HALF:BS], tail, numbers, preferred_element_type=F32)
    return top[:, 0:HALF], top[:, HALF:BS], last


def mix(*terms):
    mixed = []
    for corner in range(3):
        total = None
        for factor, corners in terms:
            value = corners[corner] if factor == 1 else factor * corners[corner]
            total = value if total is None else total + value
        mixed.append(total)
    return tuple(mixed)


def newton(currents):
    lows = [whole(m) for m in currents]
    parts = [mix((1, corners_of(low, low, 0)), (-2.5, m)) for low, m in zip(lows, currents)]
    slows = [whole(part) for part in parts]
    fourths = [whole(mix((1, corners_of(slow, slow, 0)), (3.125, part))) for slow, part in zip(slows, parts)]
    later = [mix((1, corners_of(four, low, 0)), (2.44140625, m)) for four, low, m in zip(fourths, lows, currents)]
    return later, lows


def squares(matrix):
    return jnp.sum(matrix * matrix, keepdims=True)


def oriented_into(core, dense, oriented):
    @pl.when(core == 0)
    def _():
        oriented[...] = dense[...]

    @pl.when(core == 1)
    def _():
        oriented[...] = dense[...].T


def root_kernel(got, far, stat, out, dense, oriented):
    core, _, _ = place()
    for b in BLOCKS:
        rows = slice(b * CHUNK, (b + 1) * CHUNK)
        for y in range(4):
            for where, source in ((core, got), (1 - core, far)):
                at = pl.multiple_of(where * HALF + y * CHUNK, CHUNK)
                dense[b, pl.ds(at, CHUNK), :] = source[y, rows, :]
        oriented_into(core, dense.at[b], oriented.at[b])
    sides = [oriented[b] for b in BLOCKS]
    grams = [corners_of(side, side, 1) for side in sides]
    shifted = [mix((1, tuple(stat[b, k] for k in range(3))), (1.0 - BETA, grams[b])) for b in BLOCKS]
    frobs = [jnp.sqrt(squares(m[0]) + 2.0 * squares(m[1]) + squares(m[2])) for m in shifted]
    b0 = [tuple(corner * (0.25 / frob) for corner in m) for m, frob in zip(shifted, frobs)]
    b1, low0 = newton(b0)
    b2, low1 = newton(b1)
    n01 = [mix((1, corners_of(p, q, 0)), (-1.25, u), (-1.25, v)) for p, q, u, v in zip(low0, low1, b0, b1)]
    ends = [corners_of(whole(n), whole(m), 0) for n, m in zip(n01, b2)]
    excess = [whole(mix((1.25, n), (-1.5625, m), (-1.0, end))) for n, m, end in zip(n01, b2, ends)]
    scales = [lax.rsqrt(jnp.sqrt(frob)) for frob in frobs]

    @pl.when(core == 0)
    def _():
        for b in BLOCKS:
            block = dense[b]
            value = scales[b] * (1.953125 * block.astype(F32) + mm(excess[b], block))
            out[b * BS : (b + 1) * BS, :] = value.astype(BF)
        out[2 * BS : 2 * BS + TAIL, :] = jnp.zeros((TAIL, BS), BF)

    @pl.when(core == 1)
    def _():
        line = lax.broadcasted_iota(jnp.int32, (TAIL, BS), 0)
        tail = jnp.zeros((TAIL, BS), F32)
        for b in BLOCKS:
            out[b * BS : (b + 1) * BS, :] = excess[b]
            value = jnp.broadcast_to(scales[b], (TAIL, BS))
            for term in range(3):
                high = value.astype(BF).astype(F32)
                tail = jnp.where(line == b * 8 + term, high, tail)
                value = value - high
        out[2 * BS : 2 * BS + TAIL, :] = tail.astype(BF)


def stat_kernel(owner, dense, stat, out, sums, oriented):
    core, y, half = place()
    pair = half * 4 + y
    owned = [owner_of(owner, b) == pair for b in BLOCKS]
    for b in BLOCKS:
        sums[b] = jnp.broadcast_to(squares(dense[b].astype(F32)), (8, 128))

        @pl.when(owned[b])
        def _():
            oriented_into(core, dense.at[b], oriented)
            side = oriented[...]
            gram = lax.dot_general(side, side, (((1,), (1,)), ((), ())), preferred_element_type=F32)
            out[...] = BETA * stat[...] + (1.0 - BETA) * gram

    @pl.when(jnp.logical_not(jnp.logical_or(*owned)))
    def _():
        out[...] = stat[...]


def product_kernel(mine, other, sums, out, done, sems):
    core, _, _ = place()

    def products(left, right):
        tail = right[2 * BS : 2 * BS + TAIL, :].astype(F32)
        for b in BLOCKS:
            at = b * 8
            scale = tail[at : at + 1, 0:1] + tail[at + 1 : at + 2, 0:1] + tail[at + 2 : at + 3, 0:1]
            rows = slice(b * BS, (b + 1) * BS)
            low = left[rows, :]
            precond = scale * (1.953125 * low.astype(F32) + mm(low, right[rows, :]))
            ratio = jnp.sqrt(sums[b, 0:1, 0:1] / (squares(precond) + 1e-06))
            done[b] = (precond * ratio).astype(BF)
            pltpu.make_async_copy(done.at[b], out.at[b], sems.at[b]).start()

    @pl.when(core == 0)
    def _():
        products(mine, other)

    @pl.when(core == 1)
    def _():
        products(other, mine)

    for b in BLOCKS:
        pltpu.make_async_copy(done.at[b], out.at[b], sems.at[b]).wait()


def body(grad, stats, owner):
    along_y = [[h * 8 + 2 * k + c for k in range(4)] for h in range(2) for c in range(2)]

    def send(value, bits):
        return lax.ppermute(value, "group", [(g, g ^ bits) for g in range(16)])

    def gather(value, bits):
        return lax.all_gather(value, "group", axis_index_groups=[[g, g ^ bits] for g in range(16) if g < g ^ bits])

    def exchange(value):
        return lax.all_to_all(value, "group", 0, 0, tiled=True, axis_index_groups=along_y)

    block = grad[0]
    stat = stats[0, 0]
    pieces = [call(take(other), array(2, HALF, BS), [HBM], [pltpu.SemaphoreType.DMA((2,))]) for other in (True, False)]
    got = send(pieces[0](block), 1)
    keep = pieces[1](block)
    packed = call(pack_kernel, array(4, STAT, BS), [VM], nbytes=3 << 19)(stat)
    parts = exchange(call(first_kernel, array(4, PART, BS), [VM, VM, VM, VM])(keep, got, packed, owner))
    partial = call(second_kernel, array(ROWS, BS), [VM, VM])(owner, parts)
    parts = exchange(call(third_kernel, array(4, ROWS, BS), [VM, VM])(owner, gather(partial, 8)))
    far = send(parts[:, : 2 * CHUNK], 1)
    shifted = call(unpack_kernel, array(2, 3, HALF, HALF, dtype=F32), [VM], nbytes=5 << 19)(parts)
    pair = pltpu.VMEM((2, BS, BS), BF)
    payload, dense = call(
        root_kernel, (array(2 * BS + TAIL, BS), array(2, BS, BS)), [VM, VM, VM], [pair], flops=20 * 2 * BS**3
    )(parts, far, shifted)
    received = send(payload, 1)
    new_stat, sums = call(
        stat_kernel,
        (array(BS, BS, dtype=F32), array(2, 8, 128, dtype=F32)),
        [VM, VM, VM],
        [pltpu.VMEM((BS, BS), BF)],
        flops=2 * BS**3,
        nbytes=3 << 20,
    )(owner, dense, stat)
    update = call(
        product_kernel,
        array(2, BS, BS),
        [VM, VM, VM],
        [pair, pltpu.SemaphoreType.DMA((2,))],
        flops=4 * BS**3,
        out_spec=HBM,
    )(payload, received, sums)
    return (new_stat[None, None], update)


def solution(mesh):
    in_specs = (P("group", "dp", None, None), P("group", "dp", None, None), P())
    out_specs = (P("group", "dp", None, None), P("dp", None, None))
    return jax.shard_map(body, mesh=mesh, in_specs=in_specs, out_specs=out_specs, check_vma=False)
```

```python
import jax
import jax.numpy as jnp
from jax import lax
from jax.experimental import pallas as pl
from jax.experimental.pallas import tpu as pltpu
from jax.sharding import PartitionSpec as P

BETA = 0.9
DAMPING = 0.0001
BS = 512
HALF = 256
CHUNK = 64
TILE = 8
STAT = CHUNK + TILE
PART = 2 * CHUNK + STAT
ROWS = 4 * CHUNK + TILE
TAIL = 16
PIECES = 4
LIMIT = 40 * 1024 * 1024

BF = jnp.bfloat16
F32 = jnp.float32

VM = pl.BlockSpec(memory_space=pltpu.VMEM)
HBM = pl.BlockSpec(memory_space=pl.ANY)
BLOCKS = range(2)


def call(kernel, shapes, specs, scratch=(), flops=0, nbytes=0, out_spec=VM, **more):
    many = isinstance(shapes, tuple)
    return pl.pallas_call(
        kernel,
        out_shape=shapes,
        in_specs=specs,
        out_specs=(out_spec,) * len(shapes) if many else out_spec,
        scratch_shapes=list(scratch),
        compiler_params=pltpu.CompilerParams(vmem_limit_bytes=LIMIT),
        cost_estimate=pl.CostEstimate(flops=flops, bytes_accessed=nbytes, transcendentals=0),
        **more,
    )


def array(*shape, dtype=BF):
    return jax.ShapeDtypeStruct(shape, dtype)


def place():
    group = lax.axis_index("group")
    return lax.rem(group, 2), lax.rem(lax.div(group, 2), 4), lax.div(group, 8)


def owner_of(owner, block):
    row = lax.broadcasted_iota(jnp.int32, owner.shape, 0) == lax.axis_index("dp")
    col = lax.broadcasted_iota(jnp.int32, owner.shape, 1) == block
    return jnp.sum(jnp.where(row & col, owner[...], 0))


def half_at(core):
    return pl.ds(pl.multiple_of(core * HALF, HALF), HALF)


def mm(a, b):
    return jnp.dot(a.astype(BF), b.astype(BF), preferred_element_type=F32)


def grid_of(n):
    return lax.broadcasted_iota(jnp.int32, (n, n), 0), lax.broadcasted_iota(jnp.int32, (n, n), 1)


def pack_kernel(stat, out):
    row, col = grid_of(HALF)
    corner = stat[HALF:BS, HALF:BS]
    fold = jnp.where(row <= col, stat[0:HALF, 0:HALF], corner).astype(BF)
    diagonal = jnp.sum(jnp.where(row == col, corner, 0.0), axis=0, keepdims=True)
    diagonal = jnp.broadcast_to(diagonal, (TILE, HALF)).astype(BF)
    side = stat[0:HALF, HALF:BS].astype(BF)
    for y in range(4):
        lo = y * CHUNK
        out[y, 0:CHUNK, 0:HALF] = fold[lo : lo + CHUNK]
        out[y, 0:CHUNK, HALF:BS] = side[lo : lo + CHUNK]
        out[y, CHUNK:STAT, 0:HALF] = diagonal
        out[y, CHUNK:STAT, HALF:BS] = diagonal


def first_kernel(grad, got, packed, owner, out):
    del owner
    core, _, _ = place()
    for y in range(4):
        rows = pl.ds(pl.multiple_of(core * HALF + y * CHUNK, CHUNK), CHUNK)
        for b in BLOCKS:
            total = (grad[b, rows, :].astype(F32) + got[b, rows, :].astype(F32)).astype(BF)
            out[y, b * CHUNK : (b + 1) * CHUNK, :] = total
        out[y, 2 * CHUNK : PART, :] = packed[y]


def join(first, second):
    row = lax.broadcasted_iota(jnp.int32, (TILE, BS), 0)
    return jnp.where(row < TILE // 2, first.astype(F32), second.astype(F32)).astype(BF)


def second_kernel(owner, got, out):
    total = got[0, 0 : 2 * CHUNK, :].astype(F32)
    for source in range(1, 4):
        total += got[source, 0 : 2 * CHUNK, :].astype(F32)
    out[0 : 2 * CHUNK, :] = total.astype(BF)
    source = [lax.rem(owner_of(owner, b), 4) for b in BLOCKS]
    for b in BLOCKS:
        out[(2 + b) * CHUNK : (3 + b) * CHUNK, :] = got[source[b], 2 * CHUNK : 3 * CHUNK, :]
    out[4 * CHUNK : ROWS, :] = join(*(got[source[b], 3 * CHUNK : PART, :] for b in BLOCKS))


def third_kernel(owner, got, out):
    total = (got[0, 0 : 2 * CHUNK, :].astype(F32) + got[1, 0 : 2 * CHUNK, :].astype(F32)).astype(BF)
    half = [lax.div(owner_of(owner, b), 4) for b in BLOCKS]
    stats = [got[half[b], (2 + b) * CHUNK : (3 + b) * CHUNK, :] for b in BLOCKS]
    diagonals = join(*(got[half[b], 4 * CHUNK : ROWS, :] for b in BLOCKS))
    for y in range(4):
        out[y, 0 : 2 * CHUNK, :] = total
        for b in BLOCKS:
            out[y, (2 + b) * CHUNK : (3 + b) * CHUNK, :] = stats[b]
        out[y, 4 * CHUNK : ROWS, :] = diagonals


def unpack_kernel(got, out):
    row, col = grid_of(HALF)
    damping = jnp.where(row == col, DAMPING, 0.0)
    tile = got[0, 4 * CHUNK : ROWS, 0:HALF].astype(F32)
    for b in BLOCKS:
        rows = slice((2 + b) * CHUNK, (3 + b) * CHUNK)
        packed = BETA * jnp.concatenate([got[y, rows, :] for y in range(4)], axis=0).astype(F32)
        fold = packed[:, 0:HALF]
        turned = fold.T
        at = b * (TILE // 2)
        diagonal = BETA * tile[at : at + 1, :]
        out[b, 0] = jnp.where(row <= col, fold, turned) + damping
        out[b, 1] = packed[:, HALF:BS]
        out[b, 2] = jnp.where(row > col, fold, jnp.where(row < col, turned, diagonal)) + damping


def whole(corners):
    first, side, last = (corner.astype(BF) for corner in corners)
    top = jnp.concatenate([first, side], axis=1)
    return jnp.concatenate([top, jnp.concatenate([side.T, last], axis=1)], axis=0)


def corners_of(left, right, contract):
    numbers = (((1,), (contract,)), ((), ()))
    top = lax.dot_general(left[0:HALF], right, numbers, preferred_element_type=F32)
    tail = right[:, HALF:BS] if contract == 0 else right[HALF:BS]
    last = lax.dot_general(left[HALF:BS], tail, numbers, preferred_element_type=F32)
    return top[:, 0:HALF], top[:, HALF:BS], last


def mix(*terms):
    mixed = []
    for corner in range(3):
        total = None
        for factor, corners in terms:
            value = corners[corner] if factor == 1 else factor * corners[corner]
            total = value if total is None else total + value
        mixed.append(total)
    return tuple(mixed)


def newton(currents):
    lows = [whole(m) for m in currents]
    parts = [mix((1, corners_of(low, low, 0)), (-2.5, m)) for low, m in zip(lows, currents)]
    slows = [whole(part) for part in parts]
    fourths = [whole(mix((1, corners_of(slow, slow, 0)), (3.125, part))) for slow, part in zip(slows, parts)]
    later = [mix((1, corners_of(four, low, 0)), (2.44140625, m)) for four, low, m in zip(fourths, lows, currents)]
    return later, lows


def squares(matrix):
    return jnp.sum(matrix * matrix, keepdims=True)


def oriented_into(core, dense, oriented):
    @pl.when(core == 0)
    def _():
        oriented[...] = dense[...]

    @pl.when(core == 1)
    def _():
        oriented[...] = dense[...].T


def root_kernel(got, far, stat, out, dense, oriented):
    core, _, _ = place()
    for b in BLOCKS:
        rows = slice(b * CHUNK, (b + 1) * CHUNK)
        for y in range(4):
            for where, source in ((core, got), (1 - core, far)):
                at = pl.multiple_of(where * HALF + y * CHUNK, CHUNK)
                dense[b, pl.ds(at, CHUNK), :] = source[y, rows, :]
        oriented_into(core, dense.at[b], oriented.at[b])
    sides = [oriented[b] for b in BLOCKS]
    grams = [corners_of(side, side, 1) for side in sides]
    shifted = [mix((1, tuple(stat[b, k] for k in range(3))), (1.0 - BETA, grams[b])) for b in BLOCKS]
    frobs = [jnp.sqrt(squares(m[0]) + 2.0 * squares(m[1]) + squares(m[2])) for m in shifted]
    b0 = [tuple(corner * (0.25 / frob) for corner in m) for m, frob in zip(shifted, frobs)]
    b1, low0 = newton(b0)
    b2, low1 = newton(b1)
    n01 = [mix((1, corners_of(p, q, 0)), (-1.25, u), (-1.25, v)) for p, q, u, v in zip(low0, low1, b0, b1)]
    ends = [corners_of(whole(n), whole(m), 0) for n, m in zip(n01, b2)]
    excess = [whole(mix((1.25, n), (-1.5625, m), (-1.0, end))) for n, m, end in zip(n01, b2, ends)]
    scales = [lax.rsqrt(jnp.sqrt(frob)) for frob in frobs]

    @pl.when(core == 0)
    def _():
        for b in BLOCKS:
            block = dense[b]
            value = scales[b] * (1.953125 * block.astype(F32) + mm(excess[b], block))
            out[b * BS : (b + 1) * BS, :] = value.astype(BF)
        out[2 * BS : 2 * BS + TAIL, :] = jnp.zeros((TAIL, BS), BF)

    @pl.when(core == 1)
    def _():
        line = lax.broadcasted_iota(jnp.int32, (TAIL, BS), 0)
        tail = jnp.zeros((TAIL, BS), F32)
        for b in BLOCKS:
            out[b * BS : (b + 1) * BS, :] = excess[b]
            value = jnp.broadcast_to(scales[b], (TAIL, BS))
            for term in range(3):
                high = value.astype(BF).astype(F32)
                tail = jnp.where(line == b * 8 + term, high, tail)
                value = value - high
        out[2 * BS : 2 * BS + TAIL, :] = tail.astype(BF)


def stat_kernel(owner, dense, stat, out, sums, oriented):
    core, y, half = place()
    pair = half * 4 + y
    owned = [owner_of(owner, b) == pair for b in BLOCKS]
    for b in BLOCKS:
        sums[b] = jnp.broadcast_to(squares(dense[b].astype(F32)), (8, 128))

        @pl.when(owned[b])
        def _():
            oriented_into(core, dense.at[b], oriented)
            side = oriented[...]
            gram = lax.dot_general(side, side, (((1,), (1,)), ((), ())), preferred_element_type=F32)
            out[...] = BETA * stat[...] + (1.0 - BETA) * gram

    @pl.when(jnp.logical_not(jnp.logical_or(*owned)))
    def _():
        out[...] = stat[...]


def product_kernel(mine, other, sums, out, done, sems):
    core, _, _ = place()

    def products(left, right):
        tail = right[2 * BS : 2 * BS + TAIL, :].astype(F32)
        for b in BLOCKS:
            at = b * 8
            scale = tail[at : at + 1, 0:1] + tail[at + 1 : at + 2, 0:1] + tail[at + 2 : at + 3, 0:1]
            rows = slice(b * BS, (b + 1) * BS)
            low = left[rows, :]
            precond = scale * (1.953125 * low.astype(F32) + mm(low, right[rows, :]))
            ratio = jnp.sqrt(sums[b, 0:1, 0:1] / (squares(precond) + 1e-06))
            for piece in range(PIECES):
                some = slice(piece * BS // PIECES, (piece + 1) * BS // PIECES)
                done[b, some, :] = (precond[some] * ratio).astype(BF)
                pltpu.make_async_copy(done.at[b, some, :], out.at[b, some, :], sems.at[b, piece]).start()

    @pl.when(core == 0)
    def _():
        products(mine, other)

    @pl.when(core == 1)
    def _():
        products(other, mine)

    for b in BLOCKS:
        for piece in range(PIECES):
            some = slice(piece * BS // PIECES, (piece + 1) * BS // PIECES)
            pltpu.make_async_copy(done.at[b, some, :], out.at[b, some, :], sems.at[b, piece]).wait()


def body(grad, stats, owner):
    along_y = [[h * 8 + 2 * k + c for k in range(4)] for h in range(2) for c in range(2)]

    def send(value, bits):
        return lax.ppermute(value, "group", [(g, g ^ bits) for g in range(16)])

    def gather(value, bits):
        return lax.all_gather(value, "group", axis_index_groups=[[g, g ^ bits] for g in range(16) if g < g ^ bits])

    def exchange(value):
        return lax.all_to_all(value, "group", 0, 0, tiled=True, axis_index_groups=along_y)

    block = grad[0]
    stat = stats[0, 0]
    got = send(block, 1)
    packed = call(pack_kernel, array(4, STAT, BS), [VM], nbytes=3 << 19)(stat)
    parts = exchange(call(first_kernel, array(4, PART, BS), [VM, VM, VM, VM])(block, got, packed, owner))
    partial = call(second_kernel, array(ROWS, BS), [VM, VM])(owner, parts)
    parts = exchange(call(third_kernel, array(4, ROWS, BS), [VM, VM])(owner, gather(partial, 8)))
    far = send(parts[:, : 2 * CHUNK], 1)
    shifted = call(unpack_kernel, array(2, 3, HALF, HALF, dtype=F32), [VM], nbytes=5 << 19)(parts)
    pair = pltpu.VMEM((2, BS, BS), BF)
    payload, dense = call(
        root_kernel, (array(2 * BS + TAIL, BS), array(2, BS, BS)), [VM, VM, VM], [pair], flops=20 * 2 * BS**3
    )(parts, far, shifted)
    received = send(payload, 1)
    new_stat, sums = call(
        stat_kernel,
        (array(BS, BS, dtype=F32), array(2, 8, 128, dtype=F32)),
        [VM, VM, VM],
        [pltpu.VMEM((BS, BS), BF)],
        flops=2 * BS**3,
        nbytes=3 << 20,
    )(owner, dense, stat)
    update = call(
        product_kernel,
        array(2, BS, BS),
        [VM, VM, VM],
        [pair, pltpu.SemaphoreType.DMA((2, PIECES))],
        flops=4 * BS**3,
        out_spec=HBM,
    )(payload, received, sums)
    return (new_stat[None, None], update)


def solution(mesh):
    in_specs = (P("group", "dp", None, None), P("group", "dp", None, None), P())
    out_specs = (P("group", "dp", None, None), P("dp", None, None))
    return jax.shard_map(body, mesh=mesh, in_specs=in_specs, out_specs=out_specs, check_vma=False)
```

```python
import jax
import jax.numpy as jnp
from jax import lax
from jax.experimental import pallas as pl
from jax.experimental.pallas import tpu as pltpu
from jax.sharding import PartitionSpec as P

BETA = 0.9
DAMPING = 0.0001
BS = 512
HALF = 256
CHUNK = 128
FOLD = 64
TILE = 8
STAT = FOLD + TILE
PART = CHUNK + STAT
ROWS = CHUNK + 2 * FOLD + TILE
TAIL = 16
LIMIT = 40 * 1024 * 1024

BF = jnp.bfloat16
F32 = jnp.float32

VM = pl.BlockSpec(memory_space=pltpu.VMEM)
HBM = pl.BlockSpec(memory_space=pl.ANY)
BLOCKS = range(2)


def call(kernel, shapes, specs, scratch=(), flops=0, nbytes=0, out_spec=VM, **more):
    many = isinstance(shapes, tuple)
    return pl.pallas_call(
        kernel,
        out_shape=shapes,
        in_specs=specs,
        out_specs=(out_spec,) * len(shapes) if many and not isinstance(out_spec, tuple) else out_spec,
        scratch_shapes=list(scratch),
        compiler_params=pltpu.CompilerParams(vmem_limit_bytes=LIMIT),
        cost_estimate=pl.CostEstimate(flops=flops, bytes_accessed=nbytes, transcendentals=0),
        **more,
    )


def array(*shape, dtype=BF):
    return jax.ShapeDtypeStruct(shape, dtype)


def place():
    group = lax.axis_index("group")
    return lax.rem(group, 2), lax.rem(lax.div(group, 2), 4), lax.div(group, 8)


def owner_of(owner, block):
    row = lax.broadcasted_iota(jnp.int32, owner.shape, 0) == lax.axis_index("dp")
    col = lax.broadcasted_iota(jnp.int32, owner.shape, 1) == block
    return jnp.sum(jnp.where(row & col, owner[...], 0))


def mm(a, b):
    return jnp.dot(a.astype(BF), b.astype(BF), preferred_element_type=F32)


def grid_of(n):
    return lax.broadcasted_iota(jnp.int32, (n, n), 0), lax.broadcasted_iota(jnp.int32, (n, n), 1)


def pack_kernel(stat, out):
    row, col = grid_of(HALF)
    corner = stat[HALF:BS, HALF:BS]
    fold = jnp.where(row <= col, stat[0:HALF, 0:HALF], corner).astype(BF)
    diagonal = jnp.sum(jnp.where(row == col, corner, 0.0), axis=0, keepdims=True)
    diagonal = jnp.broadcast_to(diagonal, (TILE, HALF)).astype(BF)
    side = stat[0:HALF, HALF:BS].astype(BF)
    for y in range(4):
        lo = y * FOLD
        out[y, 0:FOLD, 0:HALF] = fold[lo : lo + FOLD]
        out[y, 0:FOLD, HALF:BS] = side[lo : lo + FOLD]
        out[y, FOLD:STAT, 0:HALF] = diagonal
        out[y, FOLD:STAT, HALF:BS] = diagonal


def first_kernel(grad, got, packed, owner, out):
    del owner
    core, _, _ = place()
    for y in range(4):
        rows = slice(y * CHUNK, (y + 1) * CHUNK)
        out[y, 0:CHUNK, :] = (grad[core, rows, :].astype(F32) + got[core, rows, :].astype(F32)).astype(BF)
        out[y, CHUNK:PART, :] = packed[y]


def join(first, second):
    row = lax.broadcasted_iota(jnp.int32, (TILE, BS), 0)
    return jnp.where(row < TILE // 2, first.astype(F32), second.astype(F32)).astype(BF)


def second_kernel(owner, got, out):
    total = got[0, 0:CHUNK, :].astype(F32)
    for source in range(1, 4):
        total += got[source, 0:CHUNK, :].astype(F32)
    out[0:CHUNK, :] = total.astype(BF)
    source = [lax.rem(owner_of(owner, b), 4) for b in BLOCKS]
    for b in BLOCKS:
        out[CHUNK + b * FOLD : CHUNK + (b + 1) * FOLD, :] = got[source[b], CHUNK : CHUNK + FOLD, :]
    out[CHUNK + 2 * FOLD : ROWS, :] = join(*(got[source[b], CHUNK + FOLD : PART, :] for b in BLOCKS))


def third_kernel(owner, got, out):
    total = (got[0, 0:CHUNK, :].astype(F32) + got[1, 0:CHUNK, :].astype(F32)).astype(BF)
    half = [lax.div(owner_of(owner, b), 4) for b in BLOCKS]
    stats = [got[half[b], CHUNK + b * FOLD : CHUNK + (b + 1) * FOLD, :] for b in BLOCKS]
    diagonals = join(*(got[half[b], CHUNK + 2 * FOLD : ROWS, :] for b in BLOCKS))
    for y in range(4):
        out[y, 0:CHUNK, :] = total
        for b in BLOCKS:
            out[y, CHUNK + b * FOLD : CHUNK + (b + 1) * FOLD, :] = stats[b]
        out[y, CHUNK + 2 * FOLD : ROWS, :] = diagonals


def folded(got, block, y):
    return got[y, pl.ds(pl.multiple_of(CHUNK + block * FOLD, FOLD), FOLD), :]


def diagonal_of(got, block):
    tile = got[0, CHUNK + 2 * FOLD : ROWS, :].astype(F32)
    return jnp.where(block == 0, tile[0:1, :], tile[TILE // 2 : TILE // 2 + 1, :])


def swap_kernel(got, out):
    core, _, _ = place()
    for y in range(4):
        out[y * CHUNK : (y + 1) * CHUNK, :] = got[y, 0:CHUNK, :]
        out[BS + y * FOLD : BS + (y + 1) * FOLD, :] = folded(got, 1 - core, y)
    out[BS + 4 * FOLD : BS + 4 * FOLD + TAIL, :] = jnp.broadcast_to(diagonal_of(got, 1 - core), (TAIL, BS)).astype(BF)


def unpacked(packed, diagonal):
    row, col = grid_of(HALF)
    packed = BETA * packed.astype(F32)
    fold = packed[:, 0:HALF]
    turned = fold.T
    first = jnp.where(row <= col, fold, turned)
    last = jnp.where(row > col, fold, jnp.where(row < col, turned, BETA * diagonal[:, 0:HALF]))
    return first, packed[:, HALF:BS], last


def whole(corners):
    first, side, last = (corner.astype(BF) for corner in corners)
    top = jnp.concatenate([first, side], axis=1)
    return jnp.concatenate([top, jnp.concatenate([side.T, last], axis=1)], axis=0)


def corners_of(left, right, contract):
    numbers = (((1,), (contract,)), ((), ()))
    top = lax.dot_general(left[0:HALF], right, numbers, preferred_element_type=F32)
    tail = right[:, HALF:BS] if contract == 0 else right[HALF:BS]
    last = lax.dot_general(left[HALF:BS], tail, numbers, preferred_element_type=F32)
    return top[:, 0:HALF], top[:, HALF:BS], last


def mix(*terms):
    mixed = []
    for corner in range(3):
        total = None
        for factor, corners in terms:
            value = corners[corner] if factor == 1 else factor * corners[corner]
            total = value if total is None else total + value
        mixed.append(total)
    return tuple(mixed)


def newton(currents):
    lows = [whole(m) for m in currents]
    parts = [mix((1, corners_of(low, low, 0)), (-2.5, m)) for low, m in zip(lows, currents)]
    slows = [whole(part) for part in parts]
    fourths = [whole(mix((1, corners_of(slow, slow, 0)), (3.125, part))) for slow, part in zip(slows, parts)]
    later = [mix((1, corners_of(four, low, 0)), (2.44140625, m)) for four, low, m in zip(fourths, lows, currents)]
    return later, lows


def squares(matrix):
    return jnp.sum(matrix * matrix, keepdims=True)


def early_kernel(got, shifted, dense, sums):
    core, _, _ = place()
    for y in range(4):
        dense[y * CHUNK : (y + 1) * CHUNK, :] = got[y, 0:CHUNK, :]
    total = dense[...]
    sums[...] = jnp.broadcast_to(squares(total.astype(F32)), (8, 128))
    row, col = grid_of(HALF)
    damping = jnp.where(row == col, DAMPING, 0.0)
    for k, side in enumerate((total, total.T)):
        gram = corners_of(side, side, 1)
        shifted[k, 0] = (1.0 - BETA) * gram[0] + damping
        shifted[k, 1] = (1.0 - BETA) * gram[1]
        shifted[k, 2] = (1.0 - BETA) * gram[2] + damping
    packed = jnp.concatenate([folded(got, core, y) for y in range(4)], axis=0)
    for corner, value in enumerate(unpacked(packed, diagonal_of(got, core))):
        shifted[core, corner] += value


def root_kernel(early, far, dense, sums, out, shifted):
    core, _, _ = place()
    shifted[...] = early[...]
    diagonal = far[BS + 4 * FOLD : BS + 4 * FOLD + TAIL, :].astype(F32)[0:1, :]
    for corner, value in enumerate(unpacked(far[BS : BS + 4 * FOLD, :], diagonal)):
        shifted[1 - core, corner] += value
    sides = [tuple(shifted[k, corner] for corner in range(3)) for k in range(2)]
    frobs = [jnp.sqrt(squares(m[0]) + 2.0 * squares(m[1]) + squares(m[2])) for m in sides]
    b0 = [tuple(corner * (0.25 / frob) for corner in m) for m, frob in zip(sides, frobs)]
    b1, low0 = newton(b0)
    b2, low1 = newton(b1)
    n01 = [mix((1, corners_of(p, q, 0)), (-1.25, u), (-1.25, v)) for p, q, u, v in zip(low0, low1, b0, b1)]
    ends = [corners_of(whole(n), whole(m), 0) for n, m in zip(n01, b2)]
    left, right = [whole(mix((1.25, n), (-1.5625, m), (-1.0, end))) for n, m, end in zip(n01, b2, ends)]
    scale = lax.rsqrt(jnp.sqrt(frobs[0])) * lax.rsqrt(jnp.sqrt(frobs[1]))
    block = dense[...]
    part = 1.953125 * block.astype(F32) + mm(left, block)
    precond = 1.953125 * part + mm(part, right)
    ratio = scale * jnp.sqrt(sums[0:1, 0:1] / (scale * scale * squares(precond) + 1e-06))
    out[...] = (precond * ratio).astype(BF)


def stat_kernel(owner, dense, far, stat, mine, out, update, oriented, sem):
    core, y, half = place()
    copy = pltpu.make_async_copy(mine, update.at[core], sem)
    copy.start()
    pair = half * 4 + y
    own = owner_of(owner, core) == pair
    other = owner_of(owner, 1 - core) == pair

    @pl.when(own)
    def _():
        oriented[...] = dense[...]

    @pl.when(other)
    def _():
        oriented[...] = far[0:BS, :]

    @pl.when(core == 1)
    def _():
        oriented[...] = oriented[...].T

    active = jnp.logical_or(own, other)

    @pl.when(active)
    def _():
        side = oriented[...]
        gram = lax.dot_general(side, side, (((1,), (1,)), ((), ())), preferred_element_type=F32)
        out[...] = BETA * stat[...] + (1.0 - BETA) * gram

    @pl.when(jnp.logical_not(active))
    def _():
        out[...] = stat[...]

    copy.wait()


def last_kernel(other, begun, out, sem):
    del begun
    core, _, _ = place()
    copy = pltpu.make_async_copy(other, out.at[1 - core], sem)
    copy.start()
    copy.wait()


def body(grad, stats, owner):
    along_y = [[h * 8 + 2 * k + c for k in range(4)] for h in range(2) for c in range(2)]

    def send(value, bits):
        return lax.ppermute(value, "group", [(g, g ^ bits) for g in range(16)])

    def gather(value, bits):
        return lax.all_gather(value, "group", axis_index_groups=[[g, g ^ bits] for g in range(16) if g < g ^ bits])

    def exchange(value):
        return lax.all_to_all(value, "group", 0, 0, tiled=True, axis_index_groups=along_y)

    block = grad[0]
    stat = stats[0, 0]
    got = send(block, 1)
    packed = call(pack_kernel, array(4, STAT, BS), [VM], nbytes=3 << 19)(stat)
    parts = exchange(call(first_kernel, array(4, PART, BS), [VM, VM, VM, VM])(block, got, packed, owner))
    partial = call(second_kernel, array(ROWS, BS), [VM, VM])(owner, parts)
    parts = exchange(call(third_kernel, array(4, ROWS, BS), [VM, VM])(owner, gather(partial, 8)))
    far = send(call(swap_kernel, array(BS + 4 * FOLD + TAIL, BS), [VM])(parts), 1)
    corners = array(2, 3, HALF, HALF, dtype=F32)
    early, dense, sums = call(early_kernel, (corners, array(BS, BS), array(8, 128, dtype=F32)), [VM], flops=4 * BS**3)(parts)
    mine = call(
        root_kernel, array(BS, BS), [VM, VM, VM, VM], [pltpu.VMEM((2, 3, HALF, HALF), F32)], flops=20 * 2 * BS**3
    )(early, far, dense, sums)
    other = send(mine, 1)
    new_stat, begun = call(
        stat_kernel,
        (array(BS, BS, dtype=F32), array(2, BS, BS)),
        [VM, VM, VM, VM, VM],
        [pltpu.VMEM((BS, BS), BF), pltpu.SemaphoreType.DMA],
        flops=2 * BS**3,
        nbytes=3 << 20,
        out_spec=(VM, HBM),
    )(owner, dense, far, stat, mine)
    update = call(
        last_kernel,
        array(2, BS, BS),
        [VM, HBM],
        [pltpu.SemaphoreType.DMA],
        out_spec=HBM,
        input_output_aliases={1: 0},
    )(other, begun)
    return (new_stat[None, None], update)


def solution(mesh):
    in_specs = (P("group", "dp", None, None), P("group", "dp", None, None), P())
    out_specs = (P("group", "dp", None, None), P("dp", None, None))
    return jax.shard_map(body, mesh=mesh, in_specs=in_specs, out_specs=out_specs, check_vma=False)
```

```python
import jax
import jax.numpy as jnp
from jax import lax
from jax.experimental import pallas as pl
from jax.experimental.pallas import tpu as pltpu
from jax.sharding import PartitionSpec as P

BETA = 0.9
DAMPING = 0.0001
BS = 512
HALF = 256
CHUNK = 128
FOLD = 64
TILE = 8
STAT = FOLD + TILE
PART = CHUNK + STAT
ROWS = CHUNK + 2 * FOLD + TILE
TAIL = 16
LIMIT = 40 * 1024 * 1024

BF = jnp.bfloat16
F32 = jnp.float32

VM = pl.BlockSpec(memory_space=pltpu.VMEM)
HBM = pl.BlockSpec(memory_space=pl.ANY)
BLOCKS = range(2)


def call(kernel, shapes, specs, scratch=(), flops=0, nbytes=0, out_spec=VM, **more):
    many = isinstance(shapes, tuple)
    return pl.pallas_call(
        kernel,
        out_shape=shapes,
        in_specs=specs,
        out_specs=(out_spec,) * len(shapes) if many and not isinstance(out_spec, tuple) else out_spec,
        scratch_shapes=list(scratch),
        compiler_params=pltpu.CompilerParams(vmem_limit_bytes=LIMIT),
        cost_estimate=pl.CostEstimate(flops=flops, bytes_accessed=nbytes, transcendentals=0),
        **more,
    )


def array(*shape, dtype=BF):
    return jax.ShapeDtypeStruct(shape, dtype)


def place():
    group = lax.axis_index("group")
    return lax.rem(group, 2), lax.rem(lax.div(group, 2), 4), lax.div(group, 8)


def owner_of(owner, block):
    row = lax.broadcasted_iota(jnp.int32, owner.shape, 0) == lax.axis_index("dp")
    col = lax.broadcasted_iota(jnp.int32, owner.shape, 1) == block
    return jnp.sum(jnp.where(row & col, owner[...], 0))


def mm(a, b):
    return jnp.dot(a.astype(BF), b.astype(BF), preferred_element_type=F32)


def grid_of(n):
    return lax.broadcasted_iota(jnp.int32, (n, n), 0), lax.broadcasted_iota(jnp.int32, (n, n), 1)


def pack_kernel(stat, out):
    row, col = grid_of(HALF)
    corner = stat[HALF:BS, HALF:BS]
    fold = jnp.where(row <= col, stat[0:HALF, 0:HALF], corner).astype(BF)
    diagonal = jnp.sum(jnp.where(row == col, corner, 0.0), axis=0, keepdims=True)
    diagonal = jnp.broadcast_to(diagonal, (TILE, HALF)).astype(BF)
    side = stat[0:HALF, HALF:BS].astype(BF)
    for y in range(4):
        lo = y * FOLD
        out[y, 0:FOLD, 0:HALF] = fold[lo : lo + FOLD]
        out[y, 0:FOLD, HALF:BS] = side[lo : lo + FOLD]
        out[y, FOLD:STAT, 0:HALF] = diagonal
        out[y, FOLD:STAT, HALF:BS] = diagonal


def first_kernel(grad, got, packed, owner, out):
    del owner
    core, _, _ = place()
    for y in range(4):
        rows = slice(y * CHUNK, (y + 1) * CHUNK)
        out[y, 0:CHUNK, :] = (grad[core, rows, :].astype(F32) + got[core, rows, :].astype(F32)).astype(BF)
        out[y, CHUNK:PART, :] = packed[y]


def join(first, second):
    row = lax.broadcasted_iota(jnp.int32, (TILE, BS), 0)
    return jnp.where(row < TILE // 2, first.astype(F32), second.astype(F32)).astype(BF)


def second_kernel(owner, got, out):
    total = got[0, 0:CHUNK, :].astype(F32)
    for source in range(1, 4):
        total += got[source, 0:CHUNK, :].astype(F32)
    out[0:CHUNK, :] = total.astype(BF)
    source = [lax.rem(owner_of(owner, b), 4) for b in BLOCKS]
    for b in BLOCKS:
        out[CHUNK + b * FOLD : CHUNK + (b + 1) * FOLD, :] = got[source[b], CHUNK : CHUNK + FOLD, :]
    out[CHUNK + 2 * FOLD : ROWS, :] = join(*(got[source[b], CHUNK + FOLD : PART, :] for b in BLOCKS))


def third_kernel(owner, got, out):
    total = (got[0, 0:CHUNK, :].astype(F32) + got[1, 0:CHUNK, :].astype(F32)).astype(BF)
    half = [lax.div(owner_of(owner, b), 4) for b in BLOCKS]
    stats = [got[half[b], CHUNK + b * FOLD : CHUNK + (b + 1) * FOLD, :] for b in BLOCKS]
    diagonals = join(*(got[half[b], CHUNK + 2 * FOLD : ROWS, :] for b in BLOCKS))
    for y in range(4):
        out[y, 0:CHUNK, :] = total
        for b in BLOCKS:
            out[y, CHUNK + b * FOLD : CHUNK + (b + 1) * FOLD, :] = stats[b]
        out[y, CHUNK + 2 * FOLD : ROWS, :] = diagonals


def folded(got, block, y):
    return got[y, pl.ds(pl.multiple_of(CHUNK + block * FOLD, FOLD), FOLD), :]


def diagonal_of(got, block):
    tile = got[0, CHUNK + 2 * FOLD : ROWS, :].astype(F32)
    return jnp.where(block == 0, tile[0:1, :], tile[TILE // 2 : TILE // 2 + 1, :])


def swap_kernel(got, out):
    core, _, _ = place()
    for y in range(4):
        out[y * CHUNK : (y + 1) * CHUNK, :] = got[y, 0:CHUNK, :]
        out[BS + y * FOLD : BS + (y + 1) * FOLD, :] = folded(got, 1 - core, y)
    out[BS + 4 * FOLD : BS + 4 * FOLD + TAIL, :] = jnp.broadcast_to(diagonal_of(got, 1 - core), (TAIL, BS)).astype(BF)


def unpacked(packed, diagonal):
    row, col = grid_of(HALF)
    packed = BETA * packed.astype(F32)
    fold = packed[:, 0:HALF]
    turned = fold.T
    first = jnp.where(row <= col, fold, turned)
    last = jnp.where(row > col, fold, jnp.where(row < col, turned, BETA * diagonal[:, 0:HALF]))
    return first, packed[:, HALF:BS], last


def whole(corners):
    first, side, last = (corner.astype(BF) for corner in corners)
    top = jnp.concatenate([first, side], axis=1)
    return jnp.concatenate([top, jnp.concatenate([side.T, last], axis=1)], axis=0)


def corners_of(left, right, contract):
    numbers = (((1,), (contract,)), ((), ()))
    top = lax.dot_general(left[0:HALF], right, numbers, preferred_element_type=F32)
    tail = right[:, HALF:BS] if contract == 0 else right[HALF:BS]
    last = lax.dot_general(left[HALF:BS], tail, numbers, preferred_element_type=F32)
    return top[:, 0:HALF], top[:, HALF:BS], last


def mix(*terms):
    mixed = []
    for corner in range(3):
        total = None
        for factor, corners in terms:
            value = corners[corner] if factor == 1 else factor * corners[corner]
            total = value if total is None else total + value
        mixed.append(total)
    return tuple(mixed)


def newton(currents):
    lows = [whole(m) for m in currents]
    parts = [mix((1, corners_of(low, low, 0)), (-2.5, m)) for low, m in zip(lows, currents)]
    slows = [whole(part) for part in parts]
    fourths = [whole(mix((1, corners_of(slow, slow, 0)), (3.125, part))) for slow, part in zip(slows, parts)]
    later = [mix((1, corners_of(four, low, 0)), (2.44140625, m)) for four, low, m in zip(fourths, lows, currents)]
    return later, lows


def squares(matrix):
    return jnp.sum(matrix * matrix, keepdims=True)


def norm_of(corners):
    return jnp.sqrt(squares(corners[0]) + 2.0 * squares(corners[1]) + squares(corners[2]))


def early_kernel(got, gram, low, later, dense, sums, frob, sides):
    core, _, _ = place()
    for y in range(4):
        dense[y * CHUNK : (y + 1) * CHUNK, :] = got[y, 0:CHUNK, :]
    total = dense[...]
    sides[0] = total
    sides[1] = total.T
    row, col = grid_of(HALF)
    damping = jnp.where(row == col, DAMPING, 0.0)

    def damped(side):
        first, cross, last = corners_of(side, side, 1)
        return (1.0 - BETA) * first + damping, (1.0 - BETA) * cross, (1.0 - BETA) * last + damping

    packed = jnp.concatenate([folded(got, core, y) for y in range(4)], axis=0)
    shifted = mix((1, damped(sides[core])), (1, unpacked(packed, diagonal_of(got, core))))
    norm = norm_of(shifted)
    after, lows = newton([tuple(corner * (0.25 / norm) for corner in shifted)])
    low[...] = lows[0]
    other = damped(sides[1 - core])
    for corner in range(3):
        later[corner] = after[0][corner]
        gram[corner] = other[corner]
    frob[...] = jnp.broadcast_to(norm, (8, 128))
    sums[...] = jnp.broadcast_to(squares(total.astype(F32)), (8, 128))


def root_kernel(gram, low, later, dense, sums, frob, far, out, factors):
    core, _, _ = place()
    diagonal = far[BS + 4 * FOLD : BS + 4 * FOLD + TAIL, :].astype(F32)[0:1, :]
    given = unpacked(far[BS : BS + 4 * FOLD, :], diagonal)
    shifted = mix((1, tuple(gram[corner] for corner in range(3))), (1, given))
    norm = norm_of(shifted)
    other, lows = newton([tuple(corner * (0.25 / norm) for corner in shifted)])
    factors[0, core] = low[...]
    factors[0, 1 - core] = lows[0]
    last, lows = newton([tuple(later[corner] for corner in range(3)), other[0]])
    factors[1, core] = lows[0]
    factors[1, 1 - core] = lows[1]
    factors[2, core] = whole(last[0])
    factors[2, 1 - core] = whole(last[1])
    value = dense[...].astype(F32)
    for step in range(3):
        value = 1.25 * value - mm(factors[step, 0], value)
        value = 1.25 * value - mm(value, factors[step, 1])
    scale = lax.rsqrt(jnp.sqrt(norm)) * lax.rsqrt(jnp.sqrt(frob[0:1, 0:1]))
    ratio = scale * jnp.sqrt(sums[0:1, 0:1] / (scale * scale * squares(value) + 1e-06))
    out[...] = (value * ratio).astype(BF)


def stat_kernel(owner, dense, far, stat, mine, out, update, oriented, sem):
    core, y, half = place()
    copy = pltpu.make_async_copy(mine, update.at[core], sem)
    copy.start()
    pair = half * 4 + y
    own = owner_of(owner, core) == pair
    other = owner_of(owner, 1 - core) == pair

    @pl.when(own)
    def _():
        oriented[...] = dense[...]

    @pl.when(other)
    def _():
        oriented[...] = far[0:BS, :]

    @pl.when(core == 1)
    def _():
        oriented[...] = oriented[...].T

    active = jnp.logical_or(own, other)

    @pl.when(active)
    def _():
        side = oriented[...]
        gram = lax.dot_general(side, side, (((1,), (1,)), ((), ())), preferred_element_type=F32)
        out[...] = BETA * stat[...] + (1.0 - BETA) * gram

    @pl.when(jnp.logical_not(active))
    def _():
        out[...] = stat[...]

    copy.wait()


def last_kernel(other, begun, out, sem):
    del begun
    core, _, _ = place()
    copy = pltpu.make_async_copy(other, out.at[1 - core], sem)
    copy.start()
    copy.wait()


def body(grad, stats, owner):
    along_y = [[h * 8 + 2 * k + c for k in range(4)] for h in range(2) for c in range(2)]

    def send(value, bits):
        return lax.ppermute(value, "group", [(g, g ^ bits) for g in range(16)])

    def gather(value, bits):
        return lax.all_gather(value, "group", axis_index_groups=[[g, g ^ bits] for g in range(16) if g < g ^ bits])

    def exchange(value):
        return lax.all_to_all(value, "group", 0, 0, tiled=True, axis_index_groups=along_y)

    block = grad[0]
    stat = stats[0, 0]
    got = send(block, 1)
    packed = call(pack_kernel, array(4, STAT, BS), [VM], nbytes=3 << 19)(stat)
    parts = exchange(call(first_kernel, array(4, PART, BS), [VM, VM, VM, VM])(block, got, packed, owner))
    partial = call(second_kernel, array(ROWS, BS), [VM, VM])(owner, parts)
    parts = exchange(call(third_kernel, array(4, ROWS, BS), [VM, VM])(owner, gather(partial, 8)))
    far = send(call(swap_kernel, array(BS + 4 * FOLD + TAIL, BS), [VM])(parts), 1)
    corners = array(3, HALF, HALF, dtype=F32)
    square = array(BS, BS)
    scalar = array(8, 128, dtype=F32)
    pair = pltpu.VMEM((2, BS, BS), BF)
    early = call(early_kernel, (corners, square, corners, square, scalar, scalar), [VM], [pair], flops=8 * BS**3)(parts)
    dense = early[3]
    factors = pltpu.VMEM((3, 2, BS, BS), BF)
    mine = call(root_kernel, square, [VM] * 7, [factors], flops=20 * BS**3)(*early, far)
    other = send(mine, 1)
    new_stat, begun = call(
        stat_kernel,
        (array(BS, BS, dtype=F32), array(2, BS, BS)),
        [VM, VM, VM, VM, VM],
        [pltpu.VMEM((BS, BS), BF), pltpu.SemaphoreType.DMA],
        flops=2 * BS**3,
        nbytes=3 << 20,
        out_spec=(VM, HBM),
    )(owner, dense, far, stat, mine)
    update = call(
        last_kernel,
        array(2, BS, BS),
        [VM, HBM],
        [pltpu.SemaphoreType.DMA],
        out_spec=HBM,
        input_output_aliases={1: 0},
    )(other, begun)
    return (new_stat[None, None], update)


def solution(mesh):
    in_specs = (P("group", "dp", None, None), P("group", "dp", None, None), P())
    out_specs = (P("group", "dp", None, None), P("dp", None, None))
    return jax.shard_map(body, mesh=mesh, in_specs=in_specs, out_specs=out_specs, check_vma=False)
```

```python
import jax
import jax.numpy as jnp
from jax import lax
from jax.experimental import pallas as pl
from jax.experimental.pallas import tpu as pltpu
from jax.sharding import PartitionSpec as P

BETA = 0.9
DAMPING = 0.0001
BS = 512
HALF = 256
CHUNK = 128
FOLD = 64
TILE = 8
STAT = FOLD + TILE
PART = CHUNK + STAT
ROWS = CHUNK + 2 * FOLD + TILE
TAIL = 16
LIMIT = 40 * 1024 * 1024

BF = jnp.bfloat16
F32 = jnp.float32

VM = pl.BlockSpec(memory_space=pltpu.VMEM)
HBM = pl.BlockSpec(memory_space=pl.ANY)
BLOCKS = range(2)


def call(kernel, shapes, specs, scratch=(), flops=0, nbytes=0, out_spec=VM, **more):
    many = isinstance(shapes, tuple)
    return pl.pallas_call(
        kernel,
        out_shape=shapes,
        in_specs=specs,
        out_specs=(out_spec,) * len(shapes) if many and not isinstance(out_spec, tuple) else out_spec,
        scratch_shapes=list(scratch),
        compiler_params=pltpu.CompilerParams(vmem_limit_bytes=LIMIT),
        cost_estimate=pl.CostEstimate(flops=flops, bytes_accessed=nbytes, transcendentals=0),
        **more,
    )


def array(*shape, dtype=BF):
    return jax.ShapeDtypeStruct(shape, dtype)


def place():
    group = lax.axis_index("group")
    return lax.rem(group, 2), lax.rem(lax.div(group, 2), 4), lax.div(group, 8)


def owner_of(owner, block):
    row = lax.broadcasted_iota(jnp.int32, owner.shape, 0) == block
    col = lax.broadcasted_iota(jnp.int32, owner.shape, 1) == lax.axis_index("dp")
    return jnp.sum(jnp.where(row & col, owner[...], 0))


def mm(a, b):
    return jnp.dot(a.astype(BF), b.astype(BF), preferred_element_type=F32)


def grid_of(n):
    return lax.broadcasted_iota(jnp.int32, (n, n), 0), lax.broadcasted_iota(jnp.int32, (n, n), 1)


def pack_kernel(stat, out):
    row, col = grid_of(HALF)
    corner = stat[HALF:BS, HALF:BS]
    fold = jnp.where(row <= col, stat[0:HALF, 0:HALF], corner).astype(BF)
    diagonal = jnp.sum(jnp.where(row == col, corner, 0.0), axis=0, keepdims=True)
    diagonal = jnp.broadcast_to(diagonal, (TILE, HALF)).astype(BF)
    side = stat[0:HALF, HALF:BS].astype(BF)
    for y in range(4):
        lo = y * FOLD
        out[y, 0:FOLD, 0:HALF] = fold[lo : lo + FOLD]
        out[y, 0:FOLD, HALF:BS] = side[lo : lo + FOLD]
        out[y, FOLD:STAT, 0:HALF] = diagonal
        out[y, FOLD:STAT, HALF:BS] = diagonal


def first_kernel(grad, got, packed, owner, out):
    del owner
    core, _, _ = place()
    for y in range(4):
        rows = slice(y * CHUNK, (y + 1) * CHUNK)
        out[y, 0:CHUNK, :] = (grad[core, rows, :].astype(F32) + got[core, rows, :].astype(F32)).astype(BF)
        out[y, CHUNK:PART, :] = packed[y]


def join(first, second):
    row = lax.broadcasted_iota(jnp.int32, (TILE, BS), 0)
    return jnp.where(row < TILE // 2, first.astype(F32), second.astype(F32)).astype(BF)


def second_kernel(owner, got, out):
    total = got[0, 0:CHUNK, :].astype(F32)
    for source in range(1, 4):
        total += got[source, 0:CHUNK, :].astype(F32)
    out[0:CHUNK, :] = total.astype(BF)
    source = [lax.rem(owner_of(owner, b), 4) for b in BLOCKS]
    for b in BLOCKS:
        out[CHUNK + b * FOLD : CHUNK + (b + 1) * FOLD, :] = got[source[b], CHUNK : CHUNK + FOLD, :]
    out[CHUNK + 2 * FOLD : ROWS, :] = join(*(got[source[b], CHUNK + FOLD : PART, :] for b in BLOCKS))


def third_kernel(owner, got, out):
    total = (got[0, 0:CHUNK, :].astype(F32) + got[1, 0:CHUNK, :].astype(F32)).astype(BF)
    half = [lax.div(owner_of(owner, b), 4) for b in BLOCKS]
    stats = [got[half[b], CHUNK + b * FOLD : CHUNK + (b + 1) * FOLD, :] for b in BLOCKS]
    diagonals = join(*(got[half[b], CHUNK + 2 * FOLD : ROWS, :] for b in BLOCKS))
    for y in range(4):
        out[y, 0:CHUNK, :] = total
        for b in BLOCKS:
            out[y, CHUNK + b * FOLD : CHUNK + (b + 1) * FOLD, :] = stats[b]
        out[y, CHUNK + 2 * FOLD : ROWS, :] = diagonals


def folded(got, block, y):
    return got[y, pl.ds(pl.multiple_of(CHUNK + block * FOLD, FOLD), FOLD), :]


def diagonal_of(got, block):
    tile = got[0, CHUNK + 2 * FOLD : ROWS, :].astype(F32)
    return jnp.where(block == 0, tile[0:1, :], tile[TILE // 2 : TILE // 2 + 1, :])


def swap_kernel(got, out):
    core, _, _ = place()
    for y in range(4):
        out[y * CHUNK : (y + 1) * CHUNK, :] = got[y, 0:CHUNK, :]
        out[BS + y * FOLD : BS + (y + 1) * FOLD, :] = folded(got, 1 - core, y)
    out[BS + 4 * FOLD : BS + 4 * FOLD + TAIL, :] = jnp.broadcast_to(diagonal_of(got, 1 - core), (TAIL, BS)).astype(BF)


def unpacked(packed, diagonal):
    row, col = grid_of(HALF)
    packed = BETA * packed.astype(F32)
    fold = packed[:, 0:HALF]
    turned = fold.T
    first = jnp.where(row <= col, fold, turned)
    last = jnp.where(row > col, fold, jnp.where(row < col, turned, BETA * diagonal[:, 0:HALF]))
    return first, packed[:, HALF:BS], last


def whole(corners):
    first, side, last = (corner.astype(BF) for corner in corners)
    top = jnp.concatenate([first, side], axis=1)
    return jnp.concatenate([top, jnp.concatenate([side.T, last], axis=1)], axis=0)


def corners_of(left, right, contract):
    numbers = (((1,), (contract,)), ((), ()))
    top = lax.dot_general(left[0:HALF], right, numbers, preferred_element_type=F32)
    tail = right[:, HALF:BS] if contract == 0 else right[HALF:BS]
    last = lax.dot_general(left[HALF:BS], tail, numbers, preferred_element_type=F32)
    return top[:, 0:HALF], top[:, HALF:BS], last


def mix(*terms):
    mixed = []
    for corner in range(3):
        total = None
        for factor, corners in terms:
            value = corners[corner] if factor == 1 else factor * corners[corner]
            total = value if total is None else total + value
        mixed.append(total)
    return tuple(mixed)


def newton(currents):
    lows = [whole(m) for m in currents]
    parts = [mix((1, corners_of(low, low, 0)), (-2.5, m)) for low, m in zip(lows, currents)]
    slows = [whole(part) for part in parts]
    fourths = [whole(mix((1, corners_of(slow, slow, 0)), (3.125, part))) for slow, part in zip(slows, parts)]
    later = [mix((1, corners_of(four, low, 0)), (2.44140625, m)) for four, low, m in zip(fourths, lows, currents)]
    return later, lows


def squares(matrix):
    return jnp.sum(matrix * matrix, keepdims=True)


def norm_of(corners):
    return jnp.sqrt(squares(corners[0]) + 2.0 * squares(corners[1]) + squares(corners[2]))


def early_kernel(got, gram, low, later, dense, sums, frob, sides):
    core, _, _ = place()
    for y in range(4):
        dense[y * CHUNK : (y + 1) * CHUNK, :] = got[y, 0:CHUNK, :]
    total = dense[...]
    sides[0] = total
    sides[1] = total.T
    row, col = grid_of(HALF)
    damping = jnp.where(row == col, DAMPING, 0.0)

    def damped(side):
        first, cross, last = corners_of(side, side, 1)
        return (1.0 - BETA) * first + damping, (1.0 - BETA) * cross, (1.0 - BETA) * last + damping

    packed = jnp.concatenate([folded(got, core, y) for y in range(4)], axis=0)
    shifted = mix((1, damped(sides[core])), (1, unpacked(packed, diagonal_of(got, core))))
    norm = norm_of(shifted)
    after, lows = newton([tuple(corner * (0.25 / norm) for corner in shifted)])
    low[...] = lows[0]
    other = damped(sides[1 - core])
    for corner in range(3):
        later[corner] = after[0][corner]
        gram[corner] = other[corner]
    frob[...] = jnp.broadcast_to(norm, (8, 128))
    sums[...] = jnp.broadcast_to(squares(total.astype(F32)), (8, 128))


def root_kernel(gram, low, later, dense, sums, frob, far, out, factors):
    core, _, _ = place()
    diagonal = far[BS + 4 * FOLD : BS + 4 * FOLD + TAIL, :].astype(F32)[0:1, :]
    given = unpacked(far[BS : BS + 4 * FOLD, :], diagonal)
    shifted = mix((1, tuple(gram[corner] for corner in range(3))), (1, given))
    norm = norm_of(shifted)
    other, lows = newton([tuple(corner * (0.25 / norm) for corner in shifted)])
    factors[0, core] = low[...]
    factors[0, 1 - core] = lows[0]
    last, lows = newton([tuple(later[corner] for corner in range(3)), other[0]])
    factors[1, core] = lows[0]
    factors[1, 1 - core] = lows[1]
    factors[2, core] = whole(last[0])
    factors[2, 1 - core] = whole(last[1])
    value = dense[...].astype(F32)
    for step in range(3):
        value = 1.25 * value - mm(factors[step, 0], value)
        value = 1.25 * value - mm(value, factors[step, 1])
    scale = lax.rsqrt(jnp.sqrt(norm)) * lax.rsqrt(jnp.sqrt(frob[0:1, 0:1]))
    ratio = scale * jnp.sqrt(sums[0:1, 0:1] / (scale * scale * squares(value) + 1e-06))
    out[...] = (value * ratio).astype(BF)


def stat_kernel(owner, dense, far, stat, mine, out, update, oriented, sem):
    core, y, half = place()
    copy = pltpu.make_async_copy(mine, update.at[core], sem)
    copy.start()
    pair = half * 4 + y
    own = owner_of(owner, core) == pair
    other = owner_of(owner, 1 - core) == pair

    @pl.when(own)
    def _():
        oriented[...] = dense[...]

    @pl.when(other)
    def _():
        oriented[...] = far[0:BS, :]

    @pl.when(core == 1)
    def _():
        oriented[...] = oriented[...].T

    active = jnp.logical_or(own, other)

    @pl.when(active)
    def _():
        side = oriented[...]
        gram = lax.dot_general(side, side, (((1,), (1,)), ((), ())), preferred_element_type=F32)
        out[...] = BETA * stat[...] + (1.0 - BETA) * gram

    @pl.when(jnp.logical_not(active))
    def _():
        out[...] = stat[...]

    copy.wait()


def last_kernel(other, begun, out, sem):
    del begun
    core, _, _ = place()
    copy = pltpu.make_async_copy(other, out.at[1 - core], sem)
    copy.start()
    copy.wait()


def body(grad, stats, owner):
    along_y = [[h * 8 + 2 * k + c for k in range(4)] for h in range(2) for c in range(2)]

    def send(value, bits):
        return lax.ppermute(value, "group", [(g, g ^ bits) for g in range(16)])

    def gather(value, bits):
        return lax.all_gather(value, "group", axis_index_groups=[[g, g ^ bits] for g in range(16) if g < g ^ bits])

    def exchange(value):
        return lax.all_to_all(value, "group", 0, 0, tiled=True, axis_index_groups=along_y)

    block = grad[0]
    owner = owner.T
    stat = stats[0, 0]
    got = send(block, 1)
    packed = call(pack_kernel, array(4, STAT, BS), [VM], nbytes=3 << 19)(stat)
    parts = exchange(call(first_kernel, array(4, PART, BS), [VM, VM, VM, VM])(block, got, packed, owner))
    partial = call(second_kernel, array(ROWS, BS), [VM, VM])(owner, parts)
    parts = exchange(call(third_kernel, array(4, ROWS, BS), [VM, VM])(owner, gather(partial, 8)))
    far = send(call(swap_kernel, array(BS + 4 * FOLD + TAIL, BS), [VM])(parts), 1)
    corners = array(3, HALF, HALF, dtype=F32)
    square = array(BS, BS)
    scalar = array(8, 128, dtype=F32)
    pair = pltpu.VMEM((2, BS, BS), BF)
    early = call(early_kernel, (corners, square, corners, square, scalar, scalar), [VM], [pair], flops=8 * BS**3)(parts)
    dense = early[3]
    factors = pltpu.VMEM((3, 2, BS, BS), BF)
    mine = call(root_kernel, square, [VM] * 7, [factors], flops=20 * BS**3)(*early, far)
    other = send(mine, 1)
    new_stat, begun = call(
        stat_kernel,
        (array(BS, BS, dtype=F32), array(2, BS, BS)),
        [VM, VM, VM, VM, VM],
        [pltpu.VMEM((BS, BS), BF), pltpu.SemaphoreType.DMA],
        flops=2 * BS**3,
        nbytes=3 << 20,
        out_spec=(VM, HBM),
    )(owner, dense, far, stat, mine)
    update = call(
        last_kernel,
        array(2, BS, BS),
        [VM, HBM],
        [pltpu.SemaphoreType.DMA],
        out_spec=HBM,
        input_output_aliases={1: 0},
    )(other, begun)
    return (new_stat[None, None], update)


def solution(mesh):
    in_specs = (P("group", "dp", None, None), P("group", "dp", None, None), P())
    out_specs = (P("group", "dp", None, None), P("dp", None, None))
    return jax.shard_map(body, mesh=mesh, in_specs=in_specs, out_specs=out_specs, check_vma=False)
```

```python
import jax
import jax.numpy as jnp
from jax import lax
from jax.experimental import pallas as pl
from jax.experimental.pallas import tpu as pltpu
from jax.sharding import PartitionSpec as P

BETA = 0.9
DAMPING = 0.0001
BS = 512
HALF = 256
CHUNK = 128
FOLD = 64
TILE = 8
STAT = FOLD + TILE
PART = CHUNK + STAT
ROWS = CHUNK + 2 * FOLD + TILE
TAIL = 16
LIMIT = 40 * 1024 * 1024

BF = jnp.bfloat16
F32 = jnp.float32

VM = pl.BlockSpec(memory_space=pltpu.VMEM)
HBM = pl.BlockSpec(memory_space=pl.ANY)
BLOCKS = range(2)


def call(kernel, shapes, specs, scratch=(), flops=0, nbytes=0, out_spec=VM, **more):
    many = isinstance(shapes, tuple)
    return pl.pallas_call(
        kernel,
        out_shape=shapes,
        in_specs=specs,
        out_specs=(out_spec,) * len(shapes) if many and not isinstance(out_spec, tuple) else out_spec,
        scratch_shapes=list(scratch),
        compiler_params=pltpu.CompilerParams(vmem_limit_bytes=LIMIT),
        cost_estimate=pl.CostEstimate(flops=flops, bytes_accessed=nbytes, transcendentals=0),
        **more,
    )


def array(*shape, dtype=BF):
    return jax.ShapeDtypeStruct(shape, dtype)


def place():
    group = lax.axis_index("group")
    return lax.rem(group, 2), lax.rem(lax.div(group, 2), 4), lax.div(group, 8)


def owner_of(owner, block):
    row = lax.broadcasted_iota(jnp.int32, owner.shape, 0) == block
    col = lax.broadcasted_iota(jnp.int32, owner.shape, 1) == lax.axis_index("dp")
    return jnp.sum(jnp.where(row & col, owner[...], 0))


def mm(a, b):
    return jnp.dot(a.astype(BF), b.astype(BF), preferred_element_type=F32)


def grid_of(n):
    return lax.broadcasted_iota(jnp.int32, (n, n), 0), lax.broadcasted_iota(jnp.int32, (n, n), 1)


def pack_kernel(stat, out):
    row, col = grid_of(HALF)
    corner = stat[HALF:BS, HALF:BS]
    fold = jnp.where(row <= col, stat[0:HALF, 0:HALF], corner).astype(BF)
    diagonal = jnp.sum(jnp.where(row == col, corner, 0.0), axis=0, keepdims=True)
    diagonal = jnp.broadcast_to(diagonal, (TILE, HALF)).astype(BF)
    side = stat[0:HALF, HALF:BS].astype(BF)
    for y in range(4):
        lo = y * FOLD
        out[y, 0:FOLD, 0:HALF] = fold[lo : lo + FOLD]
        out[y, 0:FOLD, HALF:BS] = side[lo : lo + FOLD]
        out[y, FOLD:STAT, 0:HALF] = diagonal
        out[y, FOLD:STAT, HALF:BS] = diagonal


def first_kernel(grad, got, packed, owner, out):
    del owner
    core, _, _ = place()
    for y in range(4):
        rows = slice(y * CHUNK, (y + 1) * CHUNK)
        out[y, 0:CHUNK, :] = (grad[core, rows, :].astype(F32) + got[core, rows, :].astype(F32)).astype(BF)
        out[y, CHUNK:PART, :] = packed[y]


def join(first, second):
    row = lax.broadcasted_iota(jnp.int32, (TILE, BS), 0)
    return jnp.where(row < TILE // 2, first.astype(F32), second.astype(F32)).astype(BF)


def second_kernel(owner, got, out):
    total = got[0, 0:CHUNK, :].astype(F32)
    for source in range(1, 4):
        total += got[source, 0:CHUNK, :].astype(F32)
    out[0:CHUNK, :] = total.astype(BF)
    source = [lax.rem(owner_of(owner, b), 4) for b in BLOCKS]
    for b in BLOCKS:
        out[CHUNK + b * FOLD : CHUNK + (b + 1) * FOLD, :] = got[source[b], CHUNK : CHUNK + FOLD, :]
    out[CHUNK + 2 * FOLD : ROWS, :] = join(*(got[source[b], CHUNK + FOLD : PART, :] for b in BLOCKS))


def third_kernel(owner, got, out):
    total = (got[0, 0:CHUNK, :].astype(F32) + got[1, 0:CHUNK, :].astype(F32)).astype(BF)
    half = [lax.div(owner_of(owner, b), 4) for b in BLOCKS]
    stats = [got[half[b], CHUNK + b * FOLD : CHUNK + (b + 1) * FOLD, :] for b in BLOCKS]
    diagonals = join(*(got[half[b], CHUNK + 2 * FOLD : ROWS, :] for b in BLOCKS))
    for y in range(4):
        out[y, 0:CHUNK, :] = total
        for b in BLOCKS:
            out[y, CHUNK + b * FOLD : CHUNK + (b + 1) * FOLD, :] = stats[b]
        out[y, CHUNK + 2 * FOLD : ROWS, :] = diagonals


def folded(got, block, y):
    return got[y, pl.ds(pl.multiple_of(CHUNK + block * FOLD, FOLD), FOLD), :]


def diagonal_of(got, block):
    tile = got[0, CHUNK + 2 * FOLD : ROWS, :].astype(F32)
    return jnp.where(block == 0, tile[0:1, :], tile[TILE // 2 : TILE // 2 + 1, :])


def swap_kernel(got, out):
    core, _, _ = place()
    for y in range(4):
        out[y * CHUNK : (y + 1) * CHUNK, :] = got[y, 0:CHUNK, :]
        out[BS + y * FOLD : BS + (y + 1) * FOLD, :] = folded(got, 1 - core, y)
    out[BS + 4 * FOLD : BS + 4 * FOLD + TAIL, :] = jnp.broadcast_to(diagonal_of(got, 1 - core), (TAIL, BS)).astype(BF)


def unpacked(packed, diagonal):
    row, col = grid_of(HALF)
    packed = BETA * packed.astype(F32)
    fold = packed[:, 0:HALF]
    turned = fold.T
    first = jnp.where(row <= col, fold, turned)
    last = jnp.where(row > col, fold, jnp.where(row < col, turned, BETA * diagonal[:, 0:HALF]))
    return first, packed[:, HALF:BS], last


def whole(corners):
    first, side, last = (corner.astype(BF) for corner in corners)
    top = jnp.concatenate([first, side], axis=1)
    return jnp.concatenate([top, jnp.concatenate([side.T, last], axis=1)], axis=0)


def corners_of(left, right, contract):
    numbers = (((1,), (contract,)), ((), ()))
    top = lax.dot_general(left[0:HALF], right, numbers, preferred_element_type=F32)
    tail = right[:, HALF:BS] if contract == 0 else right[HALF:BS]
    last = lax.dot_general(left[HALF:BS], tail, numbers, preferred_element_type=F32)
    return top[:, 0:HALF], top[:, HALF:BS], last


def mix(*terms):
    mixed = []
    for corner in range(3):
        total = None
        for factor, corners in terms:
            value = corners[corner] if factor == 1 else factor * corners[corner]
            total = value if total is None else total + value
        mixed.append(total)
    return tuple(mixed)


def newton(currents):
    lows = [whole(m) for m in currents]
    parts = [mix((1, corners_of(low, low, 0)), (-2.5, m)) for low, m in zip(lows, currents)]
    slows = [whole(part) for part in parts]
    fourths = [whole(mix((1, corners_of(slow, slow, 0)), (3.125, part))) for slow, part in zip(slows, parts)]
    later = [mix((1, corners_of(four, low, 0)), (2.44140625, m)) for four, low, m in zip(fourths, lows, currents)]
    return later, lows


def squares(matrix):
    return jnp.sum(matrix * matrix, keepdims=True)


def norm_of(corners):
    return jnp.sqrt(squares(corners[0]) + 2.0 * squares(corners[1]) + squares(corners[2]))


def early_kernel(got, gram, low, later, dense, sums, frob, sides):
    core, _, _ = place()
    for y in range(4):
        dense[y * CHUNK : (y + 1) * CHUNK, :] = got[y, 0:CHUNK, :]
    total = dense[...]
    sides[0] = total
    sides[1] = total.T
    row, col = grid_of(HALF)
    damping = jnp.where(row == col, DAMPING, 0.0)

    def damped(side):
        first, cross, last = corners_of(side, side, 1)
        return (1.0 - BETA) * first + damping, (1.0 - BETA) * cross, (1.0 - BETA) * last + damping

    packed = jnp.concatenate([folded(got, core, y) for y in range(4)], axis=0)
    shifted = mix((1, damped(sides[core])), (1, unpacked(packed, diagonal_of(got, core))))
    norm = norm_of(shifted)
    after, lows = newton([tuple(corner * (0.25 / norm) for corner in shifted)])
    low[...] = lows[0]
    other = damped(sides[1 - core])
    for corner in range(3):
        later[corner] = after[0][corner]
        gram[corner] = other[corner]
    frob[...] = jnp.broadcast_to(norm, (8, 128))
    sums[...] = jnp.broadcast_to(squares(total.astype(F32)), (8, 128))


def root_kernel(gram, low, later, dense, sums, frob, far, out, factors):
    core, _, _ = place()
    diagonal = far[BS + 4 * FOLD : BS + 4 * FOLD + TAIL, :].astype(F32)[0:1, :]
    given = unpacked(far[BS : BS + 4 * FOLD, :], diagonal)
    shifted = mix((1, tuple(gram[corner] for corner in range(3))), (1, given))
    norm = norm_of(shifted)
    other, lows = newton([tuple(corner * (0.25 / norm) for corner in shifted)])
    factors[0, core] = low[...]
    factors[0, 1 - core] = lows[0]
    last, lows = newton([tuple(later[corner] for corner in range(3)), other[0]])
    factors[1, core] = lows[0]
    factors[1, 1 - core] = lows[1]
    factors[2, core] = whole(last[0])
    factors[2, 1 - core] = whole(last[1])
    value = dense[...].astype(F32)
    for step in range(3):
        value = 1.25 * value - mm(factors[step, 0], value)
        value = 1.25 * value - mm(value, factors[step, 1])
    scale = lax.rsqrt(jnp.sqrt(norm)) * lax.rsqrt(jnp.sqrt(frob[0:1, 0:1]))
    ratio = scale * jnp.sqrt(sums[0:1, 0:1] / (scale * scale * squares(value) + 1e-06))
    out[...] = (value * ratio).astype(BF)


def stat_kernel(owner, dense, far, stat, mine, out, update, oriented, fresh, sems):
    core, y, half = place()
    copies = [pltpu.make_async_copy(mine, update.at[core], sems.at[4])]
    copies[0].start()
    pair = half * 4 + y
    own = owner_of(owner, core) == pair
    other = owner_of(owner, 1 - core) == pair

    @pl.when(own)
    def _():
        oriented[...] = dense[...]

    @pl.when(other)
    def _():
        oriented[...] = far[0:BS, :]

    @pl.when(core == 1)
    def _():
        oriented[...] = oriented[...].T

    active = jnp.logical_or(own, other)
    for tile in range(4):
        rows = slice(tile * CHUNK, (tile + 1) * CHUNK)

        @pl.when(active)
        def _():
            numbers = (((1,), (1,)), ((), ()))
            gram = lax.dot_general(oriented[rows, :], oriented[...], numbers, preferred_element_type=F32)
            fresh[rows, :] = BETA * stat[rows, :] + (1.0 - BETA) * gram

        @pl.when(jnp.logical_not(active))
        def _():
            fresh[rows, :] = stat[rows, :]

        copies.append(pltpu.make_async_copy(fresh.at[rows, :], out.at[rows, :], sems.at[tile]))
        copies[-1].start()
    for copy in copies:
        copy.wait()


def last_kernel(other, begun, out, sem):
    del begun
    core, _, _ = place()
    copy = pltpu.make_async_copy(other, out.at[1 - core], sem)
    copy.start()
    copy.wait()


def body(grad, stats, owner):
    along_y = [[h * 8 + 2 * k + c for k in range(4)] for h in range(2) for c in range(2)]

    def send(value, bits):
        return lax.ppermute(value, "group", [(g, g ^ bits) for g in range(16)])

    def gather(value, bits):
        return lax.all_gather(value, "group", axis_index_groups=[[g, g ^ bits] for g in range(16) if g < g ^ bits])

    def exchange(value):
        return lax.all_to_all(value, "group", 0, 0, tiled=True, axis_index_groups=along_y)

    block = grad[0]
    owner = owner.T
    stat = stats[0, 0]
    got = send(block, 1)
    packed = call(pack_kernel, array(4, STAT, BS), [VM], nbytes=3 << 19)(stat)
    parts = exchange(call(first_kernel, array(4, PART, BS), [VM, VM, VM, VM])(block, got, packed, owner))
    partial = call(second_kernel, array(ROWS, BS), [VM, VM])(owner, parts)
    parts = exchange(call(third_kernel, array(4, ROWS, BS), [VM, VM])(owner, gather(partial, 8)))
    far = send(call(swap_kernel, array(BS + 4 * FOLD + TAIL, BS), [VM])(parts), 1)
    corners = array(3, HALF, HALF, dtype=F32)
    square = array(BS, BS)
    scalar = array(8, 128, dtype=F32)
    pair = pltpu.VMEM((2, BS, BS), BF)
    early = call(early_kernel, (corners, square, corners, square, scalar, scalar), [VM], [pair], flops=8 * BS**3)(parts)
    dense = early[3]
    factors = pltpu.VMEM((3, 2, BS, BS), BF)
    mine = call(root_kernel, square, [VM] * 7, [factors], flops=20 * BS**3)(*early, far)
    other = send(mine, 1)
    new_stat, begun = call(
        stat_kernel,
        (array(BS, BS, dtype=F32), array(2, BS, BS)),
        [VM, VM, VM, VM, VM],
        [pltpu.VMEM((BS, BS), BF), pltpu.VMEM((BS, BS), F32), pltpu.SemaphoreType.DMA((5,))],
        flops=2 * BS**3,
        nbytes=3 << 20,
        out_spec=(HBM, HBM),
    )(owner, dense, far, stat, mine)
    update = call(
        last_kernel,
        array(2, BS, BS),
        [VM, HBM],
        [pltpu.SemaphoreType.DMA],
        out_spec=HBM,
        input_output_aliases={1: 0},
    )(other, begun)
    return (new_stat[None, None], update)


def solution(mesh):
    in_specs = (P("group", "dp", None, None), P("group", "dp", None, None), P())
    out_specs = (P("group", "dp", None, None), P("dp", None, None))
    return jax.shard_map(body, mesh=mesh, in_specs=in_specs, out_specs=out_specs, check_vma=False)
```

```python
import jax
import jax.numpy as jnp
from jax import lax
from jax.experimental import pallas as pl
from jax.experimental.pallas import tpu as pltpu
from jax.sharding import PartitionSpec as P

BETA = 0.9
DAMPING = 0.0001
BS = 512
HALF = 256
CHUNK = 128
FOLD = 64
TILE = 8
STAT = FOLD + TILE
PART = CHUNK + STAT
ROWS = CHUNK + 2 * FOLD + TILE
TAIL = 16
LIMIT = 40 * 1024 * 1024

BF = jnp.bfloat16
F32 = jnp.float32

VM = pl.BlockSpec(memory_space=pltpu.VMEM)
HBM = pl.BlockSpec(memory_space=pl.ANY)
BLOCKS = range(2)


def call(kernel, shapes, specs, scratch=(), flops=0, nbytes=0, out_spec=VM, **more):
    many = isinstance(shapes, tuple)
    return pl.pallas_call(
        kernel,
        out_shape=shapes,
        in_specs=specs,
        out_specs=(out_spec,) * len(shapes) if many and not isinstance(out_spec, tuple) else out_spec,
        scratch_shapes=list(scratch),
        compiler_params=pltpu.CompilerParams(vmem_limit_bytes=LIMIT),
        cost_estimate=pl.CostEstimate(flops=flops, bytes_accessed=nbytes, transcendentals=0),
        **more,
    )


def array(*shape, dtype=BF):
    return jax.ShapeDtypeStruct(shape, dtype)


def place():
    group = lax.axis_index("group")
    return lax.rem(group, 2), lax.rem(lax.div(group, 2), 4), lax.div(group, 8)


def owner_of(owner, block):
    row = lax.broadcasted_iota(jnp.int32, owner.shape, 0) == block
    col = lax.broadcasted_iota(jnp.int32, owner.shape, 1) == lax.axis_index("dp")
    return jnp.sum(jnp.where(row & col, owner[...], 0))


def mm(a, b):
    return jnp.dot(a.astype(BF), b.astype(BF), preferred_element_type=F32)


def grid_of(n):
    return lax.broadcasted_iota(jnp.int32, (n, n), 0), lax.broadcasted_iota(jnp.int32, (n, n), 1)


def pack_kernel(stat, out):
    row, col = grid_of(HALF)
    corner = stat[HALF:BS, HALF:BS]
    fold = jnp.where(row <= col, stat[0:HALF, 0:HALF], corner).astype(BF)
    diagonal = jnp.sum(jnp.where(row == col, corner, 0.0), axis=0, keepdims=True)
    diagonal = jnp.broadcast_to(diagonal, (TILE, HALF)).astype(BF)
    side = stat[0:HALF, HALF:BS].astype(BF)
    for y in range(4):
        lo = y * FOLD
        out[y, 0:FOLD, 0:HALF] = fold[lo : lo + FOLD]
        out[y, 0:FOLD, HALF:BS] = side[lo : lo + FOLD]
        out[y, FOLD:STAT, 0:HALF] = diagonal
        out[y, FOLD:STAT, HALF:BS] = diagonal


def first_kernel(grad, got, packed, owner, out):
    del owner
    core, _, _ = place()
    for y in range(4):
        rows = slice(y * CHUNK, (y + 1) * CHUNK)
        out[y, 0:CHUNK, :] = (grad[core, rows, :].astype(F32) + got[core, rows, :].astype(F32)).astype(BF)
        out[y, CHUNK:PART, :] = packed[y]


def join(first, second):
    row = lax.broadcasted_iota(jnp.int32, (TILE, BS), 0)
    return jnp.where(row < TILE // 2, first.astype(F32), second.astype(F32)).astype(BF)


def second_kernel(owner, got, out):
    total = got[0, 0:CHUNK, :].astype(F32)
    for source in range(1, 4):
        total += got[source, 0:CHUNK, :].astype(F32)
    out[0:CHUNK, :] = total.astype(BF)
    source = [lax.rem(owner_of(owner, b), 4) for b in BLOCKS]
    for b in BLOCKS:
        out[CHUNK + b * FOLD : CHUNK + (b + 1) * FOLD, :] = got[source[b], CHUNK : CHUNK + FOLD, :]
    out[CHUNK + 2 * FOLD : ROWS, :] = join(*(got[source[b], CHUNK + FOLD : PART, :] for b in BLOCKS))


def third_kernel(owner, got, out):
    total = (got[0, 0:CHUNK, :].astype(F32) + got[1, 0:CHUNK, :].astype(F32)).astype(BF)
    half = [lax.div(owner_of(owner, b), 4) for b in BLOCKS]
    stats = [got[half[b], CHUNK + b * FOLD : CHUNK + (b + 1) * FOLD, :] for b in BLOCKS]
    diagonals = join(*(got[half[b], CHUNK + 2 * FOLD : ROWS, :] for b in BLOCKS))
    for y in range(4):
        out[y, 0:CHUNK, :] = total
        for b in BLOCKS:
            out[y, CHUNK + b * FOLD : CHUNK + (b + 1) * FOLD, :] = stats[b]
        out[y, CHUNK + 2 * FOLD : ROWS, :] = diagonals


def folded(got, block, y):
    return got[y, pl.ds(pl.multiple_of(CHUNK + block * FOLD, FOLD), FOLD), :]


def diagonal_of(got, block):
    tile = got[0, CHUNK + 2 * FOLD : ROWS, :].astype(F32)
    return jnp.where(block == 0, tile[0:1, :], tile[TILE // 2 : TILE // 2 + 1, :])


def swap_kernel(got, out):
    core, _, _ = place()
    for y in range(4):
        out[y * CHUNK : (y + 1) * CHUNK, :] = got[y, 0:CHUNK, :]
        out[BS + y * FOLD : BS + (y + 1) * FOLD, :] = folded(got, 1 - core, y)
    out[BS + 4 * FOLD : BS + 4 * FOLD + TAIL, :] = jnp.broadcast_to(diagonal_of(got, 1 - core), (TAIL, BS)).astype(BF)


def unpacked(packed, diagonal):
    row, col = grid_of(HALF)
    packed = BETA * packed.astype(F32)
    fold = packed[:, 0:HALF]
    turned = fold.T
    first = jnp.where(row <= col, fold, turned)
    last = jnp.where(row > col, fold, jnp.where(row < col, turned, BETA * diagonal[:, 0:HALF]))
    return first, packed[:, HALF:BS], last


def whole(corners):
    first, side, last = (corner.astype(BF) for corner in corners)
    top = jnp.concatenate([first, side], axis=1)
    return jnp.concatenate([top, jnp.concatenate([side.T, last], axis=1)], axis=0)


def corners_of(left, right, contract):
    numbers = (((1,), (contract,)), ((), ()))
    top = lax.dot_general(left[0:HALF], right, numbers, preferred_element_type=F32)
    tail = right[:, HALF:BS] if contract == 0 else right[HALF:BS]
    last = lax.dot_general(left[HALF:BS], tail, numbers, preferred_element_type=F32)
    return top[:, 0:HALF], top[:, HALF:BS], last


def mix(*terms):
    mixed = []
    for corner in range(3):
        total = None
        for factor, corners in terms:
            value = corners[corner] if factor == 1 else factor * corners[corner]
            total = value if total is None else total + value
        mixed.append(total)
    return tuple(mixed)


def newton(currents):
    lows = [whole(m) for m in currents]
    parts = [mix((1, corners_of(low, low, 0)), (-2.5, m)) for low, m in zip(lows, currents)]
    slows = [whole(part) for part in parts]
    fourths = [whole(mix((1, corners_of(slow, slow, 0)), (3.125, part))) for slow, part in zip(slows, parts)]
    later = [mix((1, corners_of(four, low, 0)), (2.44140625, m)) for four, low, m in zip(fourths, lows, currents)]
    return later, lows


def squares(matrix):
    return jnp.sum(matrix * matrix, keepdims=True)


def norm_of(corners):
    return jnp.sqrt(squares(corners[0]) + 2.0 * squares(corners[1]) + squares(corners[2]))


def early_kernel(got, gram, low, later, dense, sums, frob, sides):
    core, _, _ = place()
    for y in range(4):
        dense[y * CHUNK : (y + 1) * CHUNK, :] = got[y, 0:CHUNK, :]
    total = dense[...]
    sides[0] = total
    sides[1] = total.T
    row, col = grid_of(HALF)
    damping = jnp.where(row == col, DAMPING, 0.0)

    def damped(side):
        first, cross, last = corners_of(side, side, 1)
        return (1.0 - BETA) * first + damping, (1.0 - BETA) * cross, (1.0 - BETA) * last + damping

    packed = jnp.concatenate([folded(got, core, y) for y in range(4)], axis=0)
    shifted = mix((1, damped(sides[core])), (1, unpacked(packed, diagonal_of(got, core))))
    norm = norm_of(shifted)
    after, lows = newton([tuple(corner * (0.25 / norm) for corner in shifted)])
    low[...] = lows[0]
    other = damped(sides[1 - core])
    for corner in range(3):
        later[corner] = after[0][corner]
        gram[corner] = other[corner]
    frob[...] = jnp.broadcast_to(norm, (8, 128))
    sums[...] = jnp.broadcast_to(squares(total.astype(F32)), (8, 128))


def root_kernel(gram, low, later, dense, sums, frob, far, out, factors):
    core, _, _ = place()
    diagonal = far[BS + 4 * FOLD : BS + 4 * FOLD + TAIL, :].astype(F32)[0:1, :]
    given = unpacked(far[BS : BS + 4 * FOLD, :], diagonal)
    shifted = mix((1, tuple(gram[corner] for corner in range(3))), (1, given))
    norm = norm_of(shifted)
    other, lows = newton([tuple(corner * (0.25 / norm) for corner in shifted)])
    factors[0, core] = low[...]
    factors[0, 1 - core] = lows[0]
    last, lows = newton([tuple(later[corner] for corner in range(3)), other[0]])
    factors[1, core] = lows[0]
    factors[1, 1 - core] = lows[1]
    factors[2, core] = whole(last[0])
    factors[2, 1 - core] = whole(last[1])
    value = dense[...].astype(F32)
    for step in range(3):
        value = 1.25 * value - mm(factors[step, 0], value)
        value = 1.25 * value - mm(value, factors[step, 1])
    scale = lax.rsqrt(jnp.sqrt(norm)) * lax.rsqrt(jnp.sqrt(frob[0:1, 0:1]))
    ratio = scale * jnp.sqrt(sums[0:1, 0:1] / (scale * scale * squares(value) + 1e-06))
    out[...] = (value * ratio).astype(BF)


def stat_kernel(owner, dense, far, stat, mine, out, update, oriented, fresh, sems):
    core, y, half = place()
    copies = [pltpu.make_async_copy(mine, update.at[core], sems.at[4])]
    copies[0].start()
    pair = half * 4 + y
    own = owner_of(owner, core) == pair
    other = owner_of(owner, 1 - core) == pair

    @pl.when(own)
    def _():
        oriented[...] = dense[...]

    @pl.when(other)
    def _():
        oriented[...] = far[0:BS, :]

    @pl.when(core == 1)
    def _():
        oriented[...] = oriented[...].T

    active = jnp.logical_or(own, other)
    tiles = [slice(tile * CHUNK, (tile + 1) * CHUNK) for tile in range(4)]
    copies += [pltpu.make_async_copy(fresh.at[rows, :], out.at[rows, :], sems.at[k]) for k, rows in enumerate(tiles)]

    @pl.when(active)
    def _():
        side = oriented[...]
        gram = lax.dot_general(side, side, (((1,), (1,)), ((), ())), preferred_element_type=F32)
        for rows, copy in zip(tiles, copies[1:]):
            fresh[rows, :] = BETA * stat[rows, :] + (1.0 - BETA) * gram[rows]
            copy.start()

    @pl.when(jnp.logical_not(active))
    def _():
        for rows, copy in zip(tiles, copies[1:]):
            fresh[rows, :] = stat[rows, :]
            copy.start()

    for copy in copies:
        copy.wait()


def last_kernel(other, begun, out, sem):
    del begun
    core, _, _ = place()
    copy = pltpu.make_async_copy(other, out.at[1 - core], sem)
    copy.start()
    copy.wait()


def body(grad, stats, owner):
    along_y = [[h * 8 + 2 * k + c for k in range(4)] for h in range(2) for c in range(2)]

    def send(value, bits):
        return lax.ppermute(value, "group", [(g, g ^ bits) for g in range(16)])

    def gather(value, bits):
        return lax.all_gather(value, "group", axis_index_groups=[[g, g ^ bits] for g in range(16) if g < g ^ bits])

    def exchange(value):
        return lax.all_to_all(value, "group", 0, 0, tiled=True, axis_index_groups=along_y)

    block = grad[0]
    owner = owner.T
    stat = stats[0, 0]
    got = send(block, 1)
    packed = call(pack_kernel, array(4, STAT, BS), [VM], nbytes=3 << 19)(stat)
    parts = exchange(call(first_kernel, array(4, PART, BS), [VM, VM, VM, VM])(block, got, packed, owner))
    partial = call(second_kernel, array(ROWS, BS), [VM, VM])(owner, parts)
    parts = exchange(call(third_kernel, array(4, ROWS, BS), [VM, VM])(owner, gather(partial, 8)))
    far = send(call(swap_kernel, array(BS + 4 * FOLD + TAIL, BS), [VM])(parts), 1)
    corners = array(3, HALF, HALF, dtype=F32)
    square = array(BS, BS)
    scalar = array(8, 128, dtype=F32)
    pair = pltpu.VMEM((2, BS, BS), BF)
    early = call(early_kernel, (corners, square, corners, square, scalar, scalar), [VM], [pair], flops=8 * BS**3)(parts)
    dense = early[3]
    factors = pltpu.VMEM((3, 2, BS, BS), BF)
    mine = call(root_kernel, square, [VM] * 7, [factors], flops=20 * BS**3)(*early, far)
    other = send(mine, 1)
    new_stat, begun = call(
        stat_kernel,
        (array(BS, BS, dtype=F32), array(2, BS, BS)),
        [VM, VM, VM, VM, VM],
        [pltpu.VMEM((BS, BS), BF), pltpu.VMEM((BS, BS), F32), pltpu.SemaphoreType.DMA((5,))],
        flops=2 * BS**3,
        nbytes=3 << 20,
        out_spec=(HBM, HBM),
    )(owner, dense, far, stat, mine)
    update = call(
        last_kernel,
        array(2, BS, BS),
        [VM, HBM],
        [pltpu.SemaphoreType.DMA],
        out_spec=HBM,
        input_output_aliases={1: 0},
    )(other, begun)
    return (new_stat[None, None], update)


def solution(mesh):
    in_specs = (P("group", "dp", None, None), P("group", "dp", None, None), P())
    out_specs = (P("group", "dp", None, None), P("dp", None, None))
    return jax.shard_map(body, mesh=mesh, in_specs=in_specs, out_specs=out_specs, check_vma=False)
```
